256 devices in a mesh: tm: 8 (over z_hi, core), seq: 32 (over z_lo, y, x).
Axes of the slice: x: 4, y: 4, z: 8 (z_hi: 4, z_lo: 2; z = z_hi * 2 + z_lo), core: 2. Of those that a mesh axis runs over, the one named last changes fastest.
Arguments:
- tokens: bfloat16 [32, 1024, 1536], P('tm', 'seq'), may hold values from -6 to 6
- mod_shift: float32 [1536], replicated, may hold values from -3 to 3
- mod_scale: float32 [1536], replicated, may hold values from -3 to 3
- out_gate: float32 [1536], replicated, may hold values from -4 to 4
- w_qkv: bfloat16 [1536, 2304], replicated, may hold values from -2 to 2
- w_out: bfloat16 [768, 1536], replicated, may hold values from -0.21875 to 0.21875
- frame_time: int32 [32], P('tm'), may hold values from 0 to 31, each once
- frame_level: int32 [32], P('tm'), may hold values from 0 to 2
Outputs:
- block_out: bfloat16 [32, 1024, 1536], P('tm', 'seq')
The draws below stay inside these ranges and needn't reach their ends.
Inputs may be any that keep to these rules, and one draw needn't show every extreme that they name: `frame_time`: every time index 0 to 31 is held by exactly one slot.
All inputs are finite; a program needn't handle non-finite values.
Results may differ from the reference program's by a relative error of at most 0.008.
The reference program's roundings to bfloat16 on the way count: a program that leaves them out, or rounds other values in their place, can miss the bound.
Values may be sent and summed in bfloat16 or wider, within the bound.
No kernel may reach another device: no remote copies, remote signals or barrier semaphores. Data moves between devices by JAX's collectives and lax.ppermute only.
A program may use at most 128 MiB of HBM per device.

```python
import math
import jax
import jax.numpy as jnp
from jax import lax

D = 1536
H = 12
HD = 64
FRAMES = 32
TOKF = 1024


def draw_w_qkv(key, part):
    key = jax.random.fold_in(key, 7)
    key_base, key_gain = jax.random.split(key, 2)
    base = jnp.clip(jax.random.normal(key_base, (D, 3, H, HD), jnp.float32), -4.5, 4.5) * D ** (-0.5)
    gains = jnp.exp(jax.random.uniform(key_gain, (H,), jnp.float32, math.log(0.7), math.log(1.4)))
    query_part = base[:, 0] * gains[None, :, None]
    key_part = base[:, 1] * gains[None, :, None]
    whole = jnp.stack([query_part, key_part, base[:, 2]], axis=1)
    return jnp.clip(whole, -2.0, 2.0).reshape(D, 3 * H * HD).astype(jnp.bfloat16)


def touch_ends(entries, rng, least, top_value):
    dims = entries.shape
    place = [jax.random.randint(jax.random.fold_in(rng, axis), (), 0, dims[axis]) for axis in range(len(dims))]
    entries = entries.at[tuple(place)].set(least)
    longest = dims.index(max(dims))
    place[longest] = (place[longest] + 1) % dims[longest]
    return entries.at[tuple(place)].set(top_value)


def shard_levels(own_key, shape, cuts, least, top_value):
    def one(axis_at, parts):
        steps = jax.random.uniform(jax.random.fold_in(jax.random.fold_in(own_key, 6), axis_at), (parts,), jnp.float32, least / len(cuts), top_value / len(cuts))
        return jnp.repeat(jnp.exp(steps), shape[axis_at] // parts).reshape((-1,) + (1,) * (len(shape) - axis_at - 1))

    loudness = one(*cuts[0])
    for cut in cuts[1:]:
        loudness = loudness * one(*cut)
    return loudness


def centred(key, shape, deviation, bound, pieces=(), held_as=jnp.bfloat16):
    result = jax.random.normal(key, shape, jnp.float32) * deviation
    if len(pieces) > 0:
        result = shard_levels(key, shape, pieces, -0.22, 0.18) * result
    return jnp.clip(result, min=-bound, max=bound).astype(held_as)


def setup_inputs(seed: int = 0) -> dict:
    arg_keys = jax.random.split(jax.random.key(seed), 9)
    return {
        "tokens": centred(arg_keys[0], (FRAMES, TOKF, D), 1.0, 6.0, ((0, 8), (1, 32))),
        "mod_shift": centred(arg_keys[1], (D,), 0.5, 3.0, (), jnp.float32),
        "mod_scale": centred(arg_keys[2], (D,), 0.5, 3.0, (), jnp.float32),
        "out_gate": centred(arg_keys[3], (D,), 1.0, 4.0, (), jnp.float32),
        "w_qkv": draw_w_qkv(jax.random.fold_in(arg_keys[8], 71), 0),
        "w_out": centred(arg_keys[5], (H * HD, D), (H * HD) ** -0.5, 0.21875),
        "frame_time": jax.random.permutation(arg_keys[6], FRAMES).astype(jnp.int32),
        "frame_level": touch_ends(jax.random.randint(arg_keys[7], (FRAMES,), 0, 3), jax.random.fold_in(arg_keys[7], 1), 0, 2).astype(jnp.int32),
    }


NEG_BIG = -1e+30

def normalize(tokens, mod_shift, mod_scale):
    values = tokens.astype(jnp.float32)
    center = lax.optimization_barrier(jnp.mean(values, axis=-1, keepdims=True))
    spread = lax.optimization_barrier(jnp.mean(jnp.square(values - center), axis=-1, keepdims=True))
    scaled = (values - center) * lax.rsqrt(spread + 1e-06)
    return (scaled * (1.0 + mod_scale) + mod_shift).astype(jnp.bfloat16)

def reference(tokens, mod_shift, mod_scale, out_gate, w_qkv, w_out, frame_time, frame_level):
    frames, frame_len, width = tokens.shape
    normed = normalize(tokens, mod_shift, mod_scale).reshape(frames * frame_len, width)
    projected = jnp.dot(normed, w_qkv, preferred_element_type=jnp.float32).astype(jnp.bfloat16)
    projected = projected.reshape(frames * frame_len, 3, H, HD)
    queries = projected[:, 0]
    keys = projected[:, 1]
    values = projected[:, 2]
    limits = jnp.right_shift(jnp.int32(frame_len), 2 * frame_level).astype(jnp.int32)
    positions = jnp.arange(frame_len, dtype=jnp.int32)
    used = positions[None, :] < limits[:, None]
    key_valid = used.reshape(-1)
    key_time = jnp.repeat(frame_time, frame_len)

    def one_head(index):
        frame = (index // H).astype(jnp.int32)
        head = (index % H).astype(jnp.int32)
        block = lax.dynamic_slice_in_dim(queries, (frame * frame_len).astype(jnp.int32), frame_len, 0)
        query_head = lax.dynamic_index_in_dim(block, head, 1, keepdims=False)
        key_head = lax.dynamic_index_in_dim(keys, head, 1, keepdims=False)
        value_head = lax.dynamic_index_in_dim(values, head, 1, keepdims=False)
        scores = jnp.dot(query_head, key_head.T, preferred_element_type=jnp.float32) * HD ** (-0.5)
        now = lax.dynamic_index_in_dim(frame_time, frame, 0, keepdims=False)
        allowed = (key_valid & (key_time <= now))[None, :]
        scores = jnp.where(allowed, scores, NEG_BIG)
        top = lax.optimization_barrier(jnp.max(scores, axis=-1, keepdims=True))
        weights = jnp.where(allowed, jnp.exp(scores - top), 0.0)
        total = lax.optimization_barrier(jnp.sum(weights, axis=-1, keepdims=True))
        summed = jnp.dot(weights.astype(jnp.bfloat16), value_head, preferred_element_type=jnp.float32)
        return (summed / total).astype(jnp.bfloat16)
    heads_out = lax.map(one_head, jnp.arange(frames * H, dtype=jnp.int32))
    attn = heads_out.reshape(frames, H, frame_len, HD).transpose(0, 2, 1, 3).reshape(frames * frame_len, H * HD)
    mixed = jnp.dot(attn, w_out, preferred_element_type=jnp.float32) * out_gate
    mixed = mixed.reshape(frames, frame_len, width) * used[:, :, None].astype(jnp.float32)
    return mixed.astype(jnp.bfloat16)
```

```python
import math

import jax
import jax.numpy as jnp
from jax import lax
from jax.experimental import pallas as pl
from jax.experimental.pallas import tpu as pltpu
from jax.sharding import PartitionSpec as P

H = 12
HD = 64
GROUPS = 4
PIECES = 8
FRAMES_DEV = 4
SHARD = 32
ROWS = FRAMES_DEV * SHARD
D = 1536
TM = 8
FRAMES = TM * FRAMES_DEV
BAND = 3 * HD
STAT_ROW = BAND
KV_ROWS = 3 * ROWS
Q_ROWS = ROWS + ROWS // 2
NOTE_ROWS = 16
Q_AT = KV_ROWS + NOTE_ROWS
SUM_ROWS = 16
V_ROWS = HD + SUM_ROWS
EXCESS = 60.0
MSG_ROWS = 208
CHUNKS_TILE = 8
KEY_TILE = CHUNKS_TILE * SHARD
QUERY_TILE = PIECES * SHARD
MAX_CHUNKS = FRAMES * GROUPS
MAX_TILES = MAX_CHUNKS // CHUNKS_TILE
SCALE = HD ** (-0.5) * math.log2(math.e)
TOP_START = -1e30
MASKED = -2e30
VMEM_BYTES = 56 * 1024 * 1024
F32 = jnp.float32
BF16 = jnp.bfloat16


def lane_ids(shape):
    return lax.broadcasted_iota(jnp.int32, shape, len(shape) - 1)


def half_pair(left, right):
    return jnp.where(lane_ids(left.shape) < HD, left, right)


def project_kernel(
    times_ref, levels_ref, tokens_ref, shift_ref, scale_ref, wq_ref, wk_ref, wv_ref, kv_out, normed_ref
):
    step = pl.program_id(0)

    @pl.when(step == 0)
    def _():
        values = tokens_ref[...].astype(F32)
        center = jnp.mean(values, axis=-1, keepdims=True)
        spread = jnp.mean(jnp.square(values - center), axis=-1, keepdims=True)
        scaled = (values - center) * lax.rsqrt(spread + 1e-06)
        normed = scaled * (1.0 + scale_ref[...].reshape(1, D)) + shift_ref[...].reshape(1, D)
        normed_ref[...] = normed.astype(BF16)
        lane = lane_ids((NOTE_ROWS, 128))
        note = jnp.zeros((NOTE_ROWS, 128), jnp.int32)
        for frame in range(FRAMES_DEV):
            note = jnp.where(lane == frame, times_ref[frame], note)
            note = jnp.where(lane == FRAMES_DEV + frame, levels_ref[frame], note)
        for slot in range(GROUPS):
            kv_out[slot, KV_ROWS:Q_AT] = note.astype(F32).astype(BF16)

    normed = normed_ref[...]
    queries = jnp.dot(normed, wq_ref[...], preferred_element_type=F32)
    keys = jnp.dot(normed, wk_ref[...], preferred_element_type=F32)
    values = jnp.dot(normed, wv_ref[...], preferred_element_type=F32)
    mine = lax.axis_index("seq") // PIECES
    half = ROWS // 2
    for odd in range(2):
        slot = jnp.bitwise_xor(2 * step + odd, mine)
        pair = slice(256, 384) if odd else slice(0, 128)
        middle = slice(128, 256)
        key_mid, value_mid, query_mid = keys[:, middle], values[:, middle], queries[:, middle]
        if odd:
            third = half_pair(pltpu.roll(key_mid, HD, 1), value_mid)
            query_third = half_pair(pltpu.roll(query_mid[:half], HD, 1), query_mid[half:])
        else:
            third = half_pair(key_mid, pltpu.roll(value_mid, HD, 1))
            query_third = half_pair(query_mid[:half], pltpu.roll(query_mid[half:], HD, 1))
        kv_out[slot, :ROWS] = keys[:, pair].astype(BF16)
        kv_out[slot, ROWS : 2 * ROWS] = values[:, pair].astype(BF16)
        kv_out[slot, 2 * ROWS : KV_ROWS] = third.astype(BF16)
        kv_out[slot, Q_AT : Q_AT + ROWS] = queries[:, pair].astype(BF16)
        kv_out[slot, Q_AT + ROWS :] = query_third.astype(BF16)


def project(frame_time, frame_level, tokens, shift, scale, w_qkv):
    width = 2 * BAND
    whole = lambda *shape: pl.BlockSpec(shape, lambda j: (0,) * len(shape))
    smem = pl.BlockSpec(memory_space=pltpu.SMEM)
    return pl.pallas_call(
        project_kernel,
        out_shape=jax.ShapeDtypeStruct((GROUPS, Q_AT + Q_ROWS, 128), BF16),
        grid=(2,),
        in_specs=[
            smem,
            smem,
            whole(ROWS, D),
            whole(D),
            whole(D),
            pl.BlockSpec((D, width), lambda j: (0, j)),
            pl.BlockSpec((D, width), lambda j: (0, 2 + j)),
            pl.BlockSpec((D, width), lambda j: (0, 4 + j)),
        ],
        out_specs=whole(GROUPS, Q_AT + Q_ROWS, 128),
        scratch_shapes=[pltpu.VMEM((ROWS, D), BF16)],
        compiler_params=pltpu.CompilerParams(vmem_limit_bytes=VMEM_BYTES),
        cost_estimate=pl.CostEstimate(
            flops=2 * ROWS * D * 3 * H * HD, bytes_accessed=2 * D * 3 * H * HD, transcendentals=0
        ),
    )(frame_time, frame_level, tokens, shift, scale, w_qkv, w_qkv, w_qkv)


def attend_kernel(
    kv_own, kv_swap, kv_up, kv_down, kv_far, kv_other, q_all, out_ref,
    kv_buf, packed, v_flip, q_ext, result, stats, note_buf, notes, slot_of, count_to, sems,
):
    seq = lax.axis_index("seq")
    group, piece = seq // PIECES, seq % PIECES

    copies = [
        pltpu.make_async_copy(src, kv_buf.at[slot], sems.at[n])
        for n, (src, slot) in enumerate(
            (
                (kv_own, 0), (kv_swap, 1), (kv_down, 2), (kv_other.at[1], 3),
                (kv_far, 4), (kv_other.at[2], 5), (kv_up, 6), (kv_other.at[0], 7),
            )
        )
    ]
    for copy in copies:
        copy.start()
    for copy in copies:
        copy.wait()

    for slot in range(TM):
        note = kv_buf[slot, 0, KV_ROWS:].astype(F32).astype(jnp.int32)
        note_buf[slot : slot + 1] = note[:1]
    to_scalars = pltpu.make_async_copy(note_buf, notes, sems.at[8])
    to_scalars.start()
    to_scalars.wait()

    def time_at(i):
        return notes[i // FRAMES_DEV, i % FRAMES_DEV]

    def level_at(i):
        return notes[i // FRAMES_DEV, FRAMES_DEV + i % FRAMES_DEV]

    def note(i, carry):
        slot_of[time_at(i)] = i
        return carry

    lax.fori_loop(0, FRAMES, note, 0)

    def pack(t, used):
        at = slot_of[t]
        slot, frame = at // FRAMES_DEV, at % FRAMES_DEV
        level = level_at(at)
        here = jnp.where(level == 0, GROUPS, jnp.where((level == 1) | (piece < 2), 1, 0))

        def one(a, carry):
            for plane in range(3):
                row = pl.multiple_of(plane * ROWS + frame * SHARD, SHARD)
                packed[used + a, plane] = kv_buf[slot, jnp.bitwise_xor(a, group), pl.ds(row, SHARD)]
            return carry

        lax.fori_loop(0, here, one, 0)
        count_to[t] = used + here
        return used + here

    total = lax.fori_loop(0, FRAMES, pack, 0)
    tiles = jnp.maximum((total + CHUNKS_TILE - 1) // CHUNKS_TILE, 1)

    def clear(c, carry):
        packed[c] = jnp.zeros((3, SHARD, 128), BF16)
        return carry

    lax.fori_loop(total, tiles * CHUNKS_TILE, clear, 0)

    eye = (
        lax.broadcasted_iota(jnp.int32, (128, 128), 0) == lax.broadcasted_iota(jnp.int32, (128, 128), 1)
    ).astype(BF16)
    flip_dims = (((1,), (1,)), ((), ()))

    def flip_values(c, carry):
        tile = packed.at[pl.ds(c * CHUNKS_TILE, CHUNKS_TILE)]
        pair = tile[:, 1].reshape(KEY_TILE, 128)
        third = tile[:, 2].reshape(KEY_TILE, 128)
        pair = lax.dot_general(eye, pair, flip_dims, preferred_element_type=F32).astype(BF16)
        third = lax.dot_general(eye[HD:], third, flip_dims, preferred_element_type=F32).astype(BF16)
        for head, rows in enumerate((pair[:HD], pair[HD:], third)):
            v_flip[c, head, :HD] = rows
            v_flip[c, head, HD:] = jnp.ones((SUM_ROWS, KEY_TILE), BF16)
        return carry

    lax.fori_loop(0, tiles, flip_values, 0)

    key_row = lax.broadcasted_iota(jnp.int32, (KEY_TILE, QUERY_TILE), 0)

    def score_tile(c, head, limit=None):
        k_tile = packed[pl.ds(c * CHUNKS_TILE, CHUNKS_TILE), 2 if head == 2 else 0].reshape(KEY_TILE, 128)
        scores = lax.dot_general(k_tile, q_ext[head], flip_dims, preferred_element_type=F32) * SCALE
        return scores if limit is None else jnp.where(key_row < limit, scores, MASKED)

    def weigh(c, head, weights):
        return jnp.dot(v_flip[c, head], weights.astype(BF16), preferred_element_type=F32)

    def tall_max(scores):
        return jnp.max(scores.reshape(KEY_TILE // 8, 8, QUERY_TILE), axis=0)

    for frame in range(FRAMES_DEV):
        query_tiles = jnp.where(level_at(frame) == 0, GROUPS, 1)
        chunks = count_to[time_at(frame)]
        key_tiles = jnp.maximum((chunks + CHUNKS_TILE - 1) // CHUNKS_TILE, 1)
        last_rows = (chunks - (key_tiles - 1) * CHUNKS_TILE) * SHARD

        def one_query_tile(a, carry, frame=frame, key_tiles=key_tiles, last_rows=last_rows):
            shards = q_all.at[:, jnp.bitwise_xor(a, group)]
            pair = shards[:, SHARD * frame : SHARD * (frame + 1)].reshape(QUERY_TILE, 128).astype(F32)
            low = ROWS + SHARD * (frame % 2)
            third = shards[:, low : low + SHARD].reshape(QUERY_TILE, 128).astype(F32)
            if frame // 2:
                third = pltpu.roll(third, HD, 1)
            none = jnp.zeros_like(pair)
            q_ext[0] = half_pair(pair, none).astype(BF16)
            q_ext[1] = half_pair(none, pair).astype(BF16)
            q_ext[2] = half_pair(third, none).astype(BF16)

            def write(tops, accs):
                totals = []
                for head in range(3):
                    sums = accs[head][HD : HD + 1]
                    out = accs[head][:HD] * jnp.where(sums > 0.0, 1.0 / sums, 0.0)
                    for part in range(QUERY_TILE // 128):
                        lanes = slice(128 * part, 128 * (part + 1))
                        result[frame, 2 * a + part, HD * head : HD * (head + 1)] = out[:, lanes]
                    totals.append(sums)
                rows = jnp.concatenate(tops + totals + [jnp.zeros((2, QUERY_TILE), F32)], axis=0)
                for part in range(QUERY_TILE // 128):
                    stats[frame, 2 * a + part] = rows[:, 128 * part : 128 * (part + 1)]

            first = [score_tile(key_tiles - 1, head, last_rows) for head in range(3)]
            tops = [jnp.maximum(jnp.max(scores, axis=0, keepdims=True), TOP_START) for scores in first]
            first = [jnp.exp2(scores - top) for scores, top in zip(first, tops)]
            state = []
            for head in range(3):
                state.append(weigh(key_tiles - 1, head, first[head]))
                state.append(jnp.broadcast_to(tops[head], (8, QUERY_TILE)))

            def key_steps(count):
                def run(c, state):
                    state = list(state)
                    items = [(count * c + n, head) for n in range(count) for head in range(3)]
                    scores = [score_tile(tile, head) for tile, head in items]
                    weights = [
                        jnp.exp2(one - tops[head]).astype(BF16) for one, (_, head) in zip(scores, items)
                    ]
                    for (tile, head), one, weight in zip(items, scores, weights):
                        state[2 * head] = state[2 * head] + weigh(tile, head, weight)
                        state[2 * head + 1] = jnp.maximum(state[2 * head + 1], tall_max(one))
                    return tuple(state)

                return run

            full = key_tiles - 1
            state = lax.fori_loop(0, full // 2, key_steps(2), tuple(state))
            state = lax.fori_loop(full // 2 * 2, full, key_steps(1), state)
            write(tops, state[::2])
            over = [jnp.max(peak - top) for peak, top in zip(state[1::2], tops)]

            @pl.when(jnp.maximum(jnp.maximum(over[0], over[1]), over[2]) > EXCESS)
            def _():
                for head in range(3):
                    def one_key_tile(c, state, head=head):
                        top, acc = state
                        scores = score_tile(c, head, jnp.where(c == full, last_rows, KEY_TILE))
                        new_top = jnp.maximum(top, jnp.max(scores, axis=0, keepdims=True))
                        acc = acc * jnp.exp2(top - new_top) + weigh(c, head, jnp.exp2(scores - new_top))
                        return new_top, acc

                    top, acc = lax.fori_loop(
                        0,
                        key_tiles,
                        one_key_tile,
                        (jnp.full((1, QUERY_TILE), TOP_START, F32), jnp.zeros((V_ROWS, QUERY_TILE), F32)),
                    )
                    sums = acc[HD : HD + 1]
                    out = acc[:HD] * jnp.where(sums > 0.0, 1.0 / sums, 0.0)
                    for part in range(QUERY_TILE // 128):
                        lanes = slice(128 * part, 128 * (part + 1))
                        result[frame, 2 * a + part, HD * head : HD * (head + 1)] = out[:, lanes]
                        stats[frame, 2 * a + part, head : head + 1] = top[:, lanes]
                        stats[frame, 2 * a + part, 3 + head : 4 + head] = sums[:, lanes]

            return carry

        lax.fori_loop(0, query_tiles, one_query_tile, 0)

    per_tile = 128 // SHARD

    def one_home_tile(tile, carry):
        for sub in range(per_tile):
            home = tile * per_tile + sub

            def gather(source):
                rows = source[0, tile].shape[0]
                lane = lane_ids((rows, 128))
                made = None
                for frame in range(FRAMES_DEV):
                    shift = (SHARD * (frame - sub)) % 128
                    piece_rows = source[frame, tile]
                    if shift:
                        piece_rows = pltpu.roll(piece_rows, shift, 1)
                    made = piece_rows if made is None else jnp.where(lane >= SHARD * frame, piece_rows, made)
                return made

            out_ref[home, :BAND] = gather(result).astype(BF16)
            stat = gather(stats)
            high = stat.astype(BF16).astype(F32)
            rest = stat - high
            middle = rest.astype(BF16).astype(F32)
            low = rest - middle
            out_ref[home, BAND:] = jnp.concatenate([high, middle], axis=0).astype(BF16)
            out_ref[home, STAT_ROW + 6 : STAT_ROW + 8] = low[:2].astype(BF16)
            out_ref[home, STAT_ROW + 14 : STAT_ROW + 16] = low[2:4].astype(BF16)
        return carry

    lax.fori_loop(0, 32 // per_tile, one_home_tile, 0)


def attend(kv_parts, q_all):
    hbm = pl.BlockSpec(memory_space=pl.ANY)
    vmem = pl.BlockSpec(memory_space=pltpu.VMEM)
    return pl.pallas_call(
        attend_kernel,
        out_shape=jax.ShapeDtypeStruct((32, MSG_ROWS, 128), BF16),
        in_specs=[hbm] * 6 + [vmem],
        out_specs=vmem,
        scratch_shapes=[
            pltpu.VMEM((TM, GROUPS, KV_ROWS + NOTE_ROWS, 128), BF16),
            pltpu.VMEM((MAX_CHUNKS, 3, SHARD, 128), BF16),
            pltpu.VMEM((MAX_TILES, 3, V_ROWS, KEY_TILE), BF16),
            pltpu.VMEM((3, QUERY_TILE, 128), BF16),
            pltpu.VMEM((FRAMES_DEV, 8, BAND, 128), F32),
            pltpu.VMEM((FRAMES_DEV, 8, 8, 128), F32),
            pltpu.VMEM((TM, 128), jnp.int32),
            pltpu.SMEM((TM, 128), jnp.int32),
            pltpu.SMEM((FRAMES,), jnp.int32),
            pltpu.SMEM((FRAMES,), jnp.int32),
            pltpu.SemaphoreType.DMA((9,)),
        ],
        compiler_params=pltpu.CompilerParams(vmem_limit_bytes=VMEM_BYTES),
        cost_estimate=pl.CostEstimate(flops=10**10, bytes_accessed=10**7, transcendentals=10**7),
    )(*kv_parts, q_all)


def finish_kernel(levels_ref, home_ref, w_ref, gate_ref, out_ref, attn_ref):
    for group in range(GROUPS):
        base = 2 * BAND * (group // 2)
        if group % 2:
            places = (base + 4 * HD, base + 5 * HD, base + 3 * HD)
        else:
            places = (base, base + HD, base + 2 * HD)
        tops, totals = [], []
        for piece in range(PIECES):
            rows = home_ref[PIECES * group + piece, STAT_ROW:].astype(F32)
            high, middle = rows[:8], rows[8:]
            low = jnp.concatenate([high[6:8], middle[6:8]], axis=0)
            whole = high[:6] + middle[:6]
            tops.append(whole[:3] + low[:3])
            totals.append(whole[3:])
        best = tops[0]
        for top in tops[1:]:
            best = jnp.maximum(best, top)
        shares = [total * jnp.exp2(top - best) for top, total in zip(tops, totals)]
        norm = shares[0]
        for share in shares[1:]:
            norm = norm + share
        norm = 1.0 / norm
        shares = [share * norm for share in shares]
        for head in range(3):
            acc = None
            for piece in range(PIECES):
                part = home_ref[PIECES * group + piece, HD * head : HD * (head + 1)].astype(F32)
                part = part * shares[piece][head : head + 1]
                acc = part if acc is None else acc + part
            attn_ref[places[head] : places[head] + HD] = acc.astype(BF16)
    mixed = lax.dot_general(
        attn_ref[...], w_ref[...], (((0,), (0,)), ((), ())), preferred_element_type=F32
    ) * gate_ref[...].reshape(1, D)
    for frame in range(FRAMES_DEV):
        rows = slice(SHARD * frame, SHARD * (frame + 1))
        limit = jnp.right_shift(jnp.int32(SHARD * 32), 2 * levels_ref[frame])
        used = lax.axis_index("seq") * SHARD < limit
        out_ref[rows] = jnp.where(used, mixed[rows], 0.0).astype(BF16)


def finish(frame_level, home, w_out, gate):
    vmem = pl.BlockSpec(memory_space=pltpu.VMEM)
    return pl.pallas_call(
        finish_kernel,
        out_shape=jax.ShapeDtypeStruct((ROWS, D), BF16),
        in_specs=[pl.BlockSpec(memory_space=pltpu.SMEM), vmem, vmem, vmem],
        out_specs=vmem,
        scratch_shapes=[pltpu.VMEM((H * HD, ROWS), BF16)],
        compiler_params=pltpu.CompilerParams(vmem_limit_bytes=VMEM_BYTES),
    )(frame_level, home, w_out, gate)


def permute(x, axis, to):
    return lax.ppermute(x, axis, [(i, to(i)) for i in range(lax.axis_size(axis))])


def other_core(i):
    return i ^ 1


def along_z(k):
    return lambda i: ((i >> 1) + k) % 4 * 2 + (i & 1)


def along_x(k):
    return lambda i: (i & ~3) | ((i + k) & 3)


def forward(i):
    return along_z(-1 if i & 1 else 1)(i)


def spread_frames(x):
    core = lax.axis_index("tm") & 1
    up = permute(x, "tm", along_z(1))
    down = permute(x, "tm", along_z(-1))
    swap = permute(x, "tm", other_core)
    far = permute(jnp.where(core == 0, up, down), "tm", forward)
    other = permute(jnp.stack([up, down, far]), "tm", other_core)
    return x, swap, up, down, far, other


def to_groups(x):
    return [x[0]] + [permute(x[k], "seq", lambda i, k=k: i ^ (8 * k)) for k in range(1, GROUPS)]


def per_device(tokens, mod_shift, mod_scale, out_gate, w_qkv, w_out, frame_time, frame_level):
    message = project(frame_time, frame_level, tokens.reshape(ROWS, D), mod_shift, mod_scale, w_qkv)
    parts = to_groups(message)
    kv_block = jnp.stack([part[:Q_AT] for part in parts])
    q_block = jnp.stack([part[Q_AT:] for part in parts])
    kv_parts = spread_frames(kv_block)
    q_send = jnp.broadcast_to(q_block[None], (PIECES,) + q_block.shape)
    pieces = [list(range(PIECES * h, PIECES * (h + 1))) for h in range(GROUPS)]
    q_all = lax.all_to_all(q_send, "seq", split_axis=0, concat_axis=0, tiled=True, axis_index_groups=pieces)
    message = attend(kv_parts, q_all)
    home = lax.all_to_all(message, "seq", split_axis=0, concat_axis=0, tiled=True)
    out = finish(frame_level, home, w_out, out_gate)
    return out.reshape(FRAMES_DEV, SHARD, D)


def solution(mesh):
    placed = (P("tm", "seq", None), P(), P(), P(), P(), P(), P("tm"), P("tm"))
    return jax.shard_map(
        per_device, mesh=mesh, in_specs=placed, out_specs=P("tm", "seq", None), check_vma=False
    )
```

```python
import math

import jax
import jax.numpy as jnp
from jax import lax
from jax.experimental import pallas as pl
from jax.experimental.pallas import tpu as pltpu
from jax.sharding import PartitionSpec as P

H = 12
HD = 64
GROUPS = 4
PIECES = 8
FRAMES_DEV = 4
SHARD = 32
ROWS = FRAMES_DEV * SHARD
D = 1536
TM = 8
FRAMES = TM * FRAMES_DEV
BAND = 3 * HD
WIDE = 4
DIGITS = 5
DIGIT_BITS = 11
LOWEST = -(2.0**33)
HEAD_ROOM = 13.0
KV_ROWS = 3 * ROWS
Q_ROWS = ROWS + ROWS // 2
NOTE_ROWS = 16
Q_AT = KV_ROWS + NOTE_ROWS
SUM_ROWS = 16
V_ROWS = HD + SUM_ROWS
EXCESS = 60.0
HEAD_ROWS = HD + 8
MSG_ROWS = 3 * HEAD_ROWS
CHUNKS_TILE = 8
KEY_TILE = CHUNKS_TILE * SHARD
QUERY_TILE = PIECES * SHARD
MAX_CHUNKS = FRAMES * GROUPS
MAX_TILES = MAX_CHUNKS // CHUNKS_TILE
SCALE = HD ** (-0.5) * math.log2(math.e)
TOP_START = -1e30
MASKED = -2e30
VMEM_BYTES = 56 * 1024 * 1024
F32 = jnp.float32
BF16 = jnp.bfloat16


def lane_ids(shape):
    return lax.broadcasted_iota(jnp.int32, shape, len(shape) - 1)


def half_pair(left, right):
    return jnp.where(lane_ids(left.shape) < HD, left, right)


def project_kernel(
    times_ref, levels_ref, tokens_ref, shift_ref, scale_ref, wq_ref, wk_ref, wv_ref, kv_out, normed_ref
):
    step = pl.program_id(0)

    @pl.when(step == 0)
    def _():
        values = tokens_ref[...].astype(F32)
        center = jnp.mean(values, axis=-1, keepdims=True)
        spread = jnp.mean(jnp.square(values - center), axis=-1, keepdims=True)
        scaled = (values - center) * lax.rsqrt(spread + 1e-06)
        normed = scaled * (1.0 + scale_ref[...].reshape(1, D)) + shift_ref[...].reshape(1, D)
        normed_ref[...] = normed.astype(BF16)
        lane = lane_ids((NOTE_ROWS, 128))
        note = jnp.zeros((NOTE_ROWS, 128), jnp.int32)
        for frame in range(FRAMES_DEV):
            note = jnp.where(lane == frame, times_ref[frame], note)
            note = jnp.where(lane == FRAMES_DEV + frame, levels_ref[frame], note)
        for slot in range(GROUPS):
            kv_out[slot, KV_ROWS:Q_AT] = note.astype(F32).astype(BF16)

    normed = normed_ref[...]
    queries = jnp.dot(normed, wq_ref[...], preferred_element_type=F32)
    keys = jnp.dot(normed, wk_ref[...], preferred_element_type=F32)
    values = jnp.dot(normed, wv_ref[...], preferred_element_type=F32)
    mine = lax.axis_index("seq") // PIECES
    half = ROWS // 2
    for odd in range(2):
        slot = jnp.bitwise_xor(2 * step + odd, mine)
        pair = slice(256, 384) if odd else slice(0, 128)
        middle = slice(128, 256)
        key_mid, value_mid, query_mid = keys[:, middle], values[:, middle], queries[:, middle]
        if odd:
            third = half_pair(pltpu.roll(key_mid, HD, 1), value_mid)
            query_third = half_pair(pltpu.roll(query_mid[:half], HD, 1), query_mid[half:])
        else:
            third = half_pair(key_mid, pltpu.roll(value_mid, HD, 1))
            query_third = half_pair(query_mid[:half], pltpu.roll(query_mid[half:], HD, 1))
        kv_out[slot, :ROWS] = keys[:, pair].astype(BF16)
        kv_out[slot, ROWS : 2 * ROWS] = values[:, pair].astype(BF16)
        kv_out[slot, 2 * ROWS : KV_ROWS] = third.astype(BF16)
        kv_out[slot, Q_AT : Q_AT + ROWS] = queries[:, pair].astype(BF16)
        kv_out[slot, Q_AT + ROWS :] = query_third.astype(BF16)


def project(frame_time, frame_level, tokens, shift, scale, w_qkv):
    width = 2 * BAND
    whole = lambda *shape: pl.BlockSpec(shape, lambda j: (0,) * len(shape))
    smem = pl.BlockSpec(memory_space=pltpu.SMEM)
    return pl.pallas_call(
        project_kernel,
        out_shape=jax.ShapeDtypeStruct((GROUPS, Q_AT + Q_ROWS, 128), BF16),
        grid=(2,),
        in_specs=[
            smem,
            smem,
            whole(ROWS, D),
            whole(D),
            whole(D),
            pl.BlockSpec((D, width), lambda j: (0, j)),
            pl.BlockSpec((D, width), lambda j: (0, 2 + j)),
            pl.BlockSpec((D, width), lambda j: (0, 4 + j)),
        ],
        out_specs=whole(GROUPS, Q_AT + Q_ROWS, 128),
        scratch_shapes=[pltpu.VMEM((ROWS, D), BF16)],
        compiler_params=pltpu.CompilerParams(vmem_limit_bytes=VMEM_BYTES),
        cost_estimate=pl.CostEstimate(
            flops=2 * ROWS * D * 3 * H * HD, bytes_accessed=2 * D * 3 * H * HD, transcendentals=0
        ),
    )(frame_time, frame_level, tokens, shift, scale, w_qkv, w_qkv, w_qkv)


def attend_kernel(*refs):
    kv_parts, q_parts, out_ref = refs[:TM], refs[TM : TM + 4], refs[TM + 4]
    kv_buf, q_buf, packed, v_flip, q_ext, excess, note_buf, notes, slot_of, place, count_to, sems, notes_vmem = refs[TM + 5 :]
    seq = lax.axis_index("seq")
    group, piece = seq // PIECES, seq % PIECES
    y_low, x_at = piece // 4, piece % 4

    note_copies = [
        pltpu.make_async_copy(kv_parts[n].at[0, KV_ROWS:Q_AT], note_buf.at[n], sems.at[n]) for n in range(TM)
    ]
    kv_copies = [pltpu.make_async_copy(kv_parts[n], kv_buf.at[n], sems.at[TM + n]) for n in range(TM)]
    q_copies = []
    for n, part in enumerate(q_parts):
        from_x = jnp.bitwise_and(x_at - n, 3)
        for flip in range(2):
            to = 4 * jnp.bitwise_xor(y_low, flip) + from_x
            q_copies.append(pltpu.make_async_copy(part.at[flip], q_buf.at[to], sems.at[2 * TM + 2 * n + flip]))
    for copy in note_copies + kv_copies + q_copies:
        copy.start()
    for copy in note_copies:
        copy.wait()
    kept = [note_buf[n].astype(F32).astype(jnp.int32)[:1] for n in range(TM)]
    notes_vmem[...] = jnp.concatenate(kept, axis=0)
    to_scalars = pltpu.make_async_copy(notes_vmem, notes, sems.at[4 * TM])
    to_scalars.start()
    to_scalars.wait()

    def time_at(i):
        return notes[i // FRAMES_DEV, i % FRAMES_DEV]

    def level_at(i):
        return notes[i // FRAMES_DEV, FRAMES_DEV + i % FRAMES_DEV]

    def chunks_of(level):
        return jnp.where(level == 0, GROUPS, jnp.where((level == 1) | (piece < 2), 1, 0))

    for i in range(FRAMES):
        slot_of[time_at(i)] = i

    def lay_out(t, used):
        i = slot_of[t]
        place[i] = used
        used = used + chunks_of(level_at(i))
        count_to[i] = used
        return used

    total = lax.fori_loop(0, FRAMES, lay_out, 0)
    tiles = jnp.maximum((total + CHUNKS_TILE - 1) // CHUNKS_TILE, 1)
    wide = (tiles + WIDE - 1) // WIDE

    def clear(c, carry):
        packed[c] = jnp.zeros((3, SHARD, 128), BF16)
        return carry

    lax.fori_loop(total, wide * WIDE * CHUNKS_TILE, clear, 0)

    for slot in range(TM):
        kv_copies[slot].wait()
        for frame in range(FRAMES_DEV):
            i = slot * FRAMES_DEV + frame
            to, here = place[i], chunks_of(level_at(i))

            def move(a, slot=slot, frame=frame, to=to):
                for plane in range(3):
                    row = plane * ROWS + frame * SHARD
                    packed[to + a, plane] = kv_buf[slot, jnp.bitwise_xor(a, group), row : row + SHARD]

            @pl.when(here > 0)
            def _(move=move):
                move(0)

            @pl.when(here > 1)
            def _(move=move):
                for a in range(1, GROUPS):
                    move(a)

    eye = (
        lax.broadcasted_iota(jnp.int32, (128, 128), 0) == lax.broadcasted_iota(jnp.int32, (128, 128), 1)
    ).astype(BF16)
    flip_dims = (((1,), (1,)), ((), ()))

    def flip_values(w, largest):
        tile = packed.at[pl.ds(w * WIDE * CHUNKS_TILE, WIDE * CHUNKS_TILE)]
        pair = lax.dot_general(
            eye, tile[:, 1].reshape(WIDE * KEY_TILE, 128), flip_dims, preferred_element_type=F32
        )
        third = lax.dot_general(
            eye[HD:], tile[:, 2].reshape(WIDE * KEY_TILE, 128), flip_dims, preferred_element_type=F32
        )
        for head, rows in enumerate((pair[:HD], pair[HD:], third)):
            for n in range(WIDE):
                part = rows[:, n * KEY_TILE : (n + 1) * KEY_TILE]
                v_flip[w * WIDE + n, head, :HD] = part.astype(BF16)
                v_flip[w * WIDE + n, head, HD:] = jnp.ones((SUM_ROWS, KEY_TILE), BF16)
                largest = jnp.maximum(largest, jnp.abs(part))
        return largest

    largest = lax.fori_loop(0, wide, flip_values, jnp.zeros((HD, KEY_TILE), F32))
    largest = jnp.max(jnp.max(largest, axis=0, keepdims=True), axis=1, keepdims=True)
    power = jnp.clip(jnp.floor(jnp.log2(largest)), -100.0, 100.0)
    grow = jnp.exp2(HEAD_ROOM - power)
    for copy in q_copies:
        copy.wait()
    excess[...] = jnp.zeros((8, QUERY_TILE), F32)

    key_row = lax.broadcasted_iota(jnp.int32, (KEY_TILE, QUERY_TILE), 0)

    def score_tile(c, head, limit=None):
        k_tile = packed[pl.ds(c * CHUNKS_TILE, CHUNKS_TILE), 2 if head == 2 else 0].reshape(KEY_TILE, 128)
        scores = lax.dot_general(k_tile, q_ext[head], flip_dims, preferred_element_type=F32) * SCALE
        return scores if limit is None else jnp.where(key_row < limit, scores, MASKED)

    def weigh(c, head, weights):
        return jnp.dot(v_flip[c, head], weights.astype(BF16), preferred_element_type=F32)

    def tall_max(scores):
        return jnp.max(scores.reshape(KEY_TILE // 8, 8, QUERY_TILE), axis=0)

    def place_queries(a, frame):
        shards = q_buf.at[:, jnp.bitwise_xor(a, group)]
        pair = shards[:, SHARD * frame : SHARD * (frame + 1)].reshape(QUERY_TILE, 128).astype(F32)
        low = ROWS + SHARD * (frame % 2)
        third = shards[:, low : low + SHARD].reshape(QUERY_TILE, 128).astype(F32)
        if frame // 2:
            third = pltpu.roll(third, HD, 1)
        none = jnp.zeros_like(pair)
        q_ext[0] = half_pair(pair, none).astype(BF16)
        q_ext[1] = half_pair(none, pair).astype(BF16)
        q_ext[2] = half_pair(third, none).astype(BF16)

    def write(a, frame, head, top, acc):
        sums = acc[HD : HD + 1]
        some = sums > 0.0
        out = acc[:HD] * jnp.where(some, grow / sums, 0.0)
        rest = jnp.where(some, top + jnp.log2(sums), LOWEST)
        digits = []
        for digit in range(DIGITS):
            unit = 2.0 ** (DIGIT_BITS * (2 - digit))
            whole = jnp.floor(rest * (1.0 / unit) + 0.5)
            rest = rest - whole * unit
            digits.append(whole)
        digits += [jnp.broadcast_to(power, (1, QUERY_TILE))] + [jnp.zeros_like(rest)] * 2
        rows = jnp.concatenate([out] + digits, axis=0)
        lanes = slice(SHARD * frame, SHARD * (frame + 1))
        for part in range(QUERY_TILE // 128):
            block = rows[:, 128 * part : 128 * (part + 1)]
            for sub in range(128 // SHARD):
                shift = (SHARD * (frame - sub)) % 128
                turned = pltpu.roll(block, shift, 1) if shift else block
                home = PIECES * a + 128 // SHARD * part + sub
                out_ref[home, HEAD_ROWS * head : HEAD_ROWS * (head + 1), lanes] = turned[:, lanes]

    def plan(frame):
        query_tiles = jnp.where(level_at(frame) == 0, GROUPS, 1)
        chunks = count_to[frame]
        key_tiles = jnp.maximum((chunks + CHUNKS_TILE - 1) // CHUNKS_TILE, 1)
        return query_tiles, key_tiles, (chunks - (key_tiles - 1) * CHUNKS_TILE) * SHARD

    for frame in range(FRAMES_DEV):
        query_tiles, key_tiles, last_rows = plan(frame)

        def one_query_tile(a, carry, frame=frame, key_tiles=key_tiles, last_rows=last_rows):
            place_queries(a, frame)
            full = key_tiles - 1
            first = [score_tile(full, head, last_rows) for head in range(3)]
            tops = [jnp.maximum(jnp.max(scores, axis=0, keepdims=True), TOP_START) for scores in first]
            first = [jnp.exp2(scores - top) for scores, top in zip(first, tops)]
            state = []
            for head in range(3):
                state.append(weigh(full, head, first[head]))
                state.append(jnp.broadcast_to(tops[head], (8, QUERY_TILE)))

            def key_steps(count):
                def run(c, state):
                    state = list(state)
                    items = [(count * c + n, head) for n in range(count) for head in range(3)]
                    scores = [score_tile(tile, head) for tile, head in items]
                    weights = [
                        jnp.exp2(one - tops[head]).astype(BF16) for one, (_, head) in zip(scores, items)
                    ]
                    for (tile, head), one, weight in zip(items, scores, weights):
                        state[2 * head] = state[2 * head] + weigh(tile, head, weight)
                        state[2 * head + 1] = jnp.maximum(state[2 * head + 1], tall_max(one))
                    return tuple(state)

                return run

            state = lax.fori_loop(0, full // 2, key_steps(2), tuple(state))
            state = lax.fori_loop(full // 2 * 2, full, key_steps(1), state)
            over = excess[...]
            for head in range(3):
                write(a, frame, head, tops[head], state[2 * head])
                over = jnp.maximum(over, state[2 * head + 1] - tops[head])
            excess[...] = over
            return carry

        lax.fori_loop(0, query_tiles, one_query_tile, 0)

    @pl.when(jnp.max(excess[...]) > EXCESS)
    def _():
        for frame in range(FRAMES_DEV):
            query_tiles, key_tiles, last_rows = plan(frame)

            def redo(a, carry, frame=frame, key_tiles=key_tiles, last_rows=last_rows):
                place_queries(a, frame)
                for head in range(3):

                    def one_key_tile(c, state, head=head):
                        top, acc = state
                        scores = score_tile(c, head, jnp.where(c == key_tiles - 1, last_rows, KEY_TILE))
                        new_top = jnp.maximum(top, jnp.max(scores, axis=0, keepdims=True))
                        acc = acc * jnp.exp2(top - new_top) + weigh(c, head, jnp.exp2(scores - new_top))
                        return new_top, acc

                    start = (jnp.full((1, QUERY_TILE), TOP_START, F32), jnp.zeros((V_ROWS, QUERY_TILE), F32))
                    top, acc = lax.fori_loop(0, key_tiles, one_key_tile, start)
                    write(a, frame, head, top, acc)
                return carry

            lax.fori_loop(0, query_tiles, redo, 0)


def attend(kv_parts, q_parts):
    hbm = pl.BlockSpec(memory_space=pl.ANY)
    vmem = pl.BlockSpec(memory_space=pltpu.VMEM)
    return pl.pallas_call(
        attend_kernel,
        out_shape=jax.ShapeDtypeStruct((32, MSG_ROWS, 128), F32),
        in_specs=[hbm] * (TM + 4),
        out_specs=vmem,
        scratch_shapes=[
            pltpu.VMEM((TM, GROUPS, Q_AT, 128), BF16),
            pltpu.VMEM((PIECES, GROUPS, Q_ROWS, 128), BF16),
            pltpu.VMEM((MAX_CHUNKS, 3, SHARD, 128), BF16),
            pltpu.VMEM((MAX_TILES, 3, V_ROWS, KEY_TILE), BF16),
            pltpu.VMEM((3, QUERY_TILE, 128), BF16),
            pltpu.VMEM((8, QUERY_TILE), F32),
            pltpu.VMEM((TM, NOTE_ROWS, 128), BF16),
            pltpu.SMEM((TM, 128), jnp.int32),
            pltpu.SMEM((FRAMES,), jnp.int32),
            pltpu.SMEM((FRAMES,), jnp.int32),
            pltpu.SMEM((FRAMES,), jnp.int32),
            pltpu.SemaphoreType.DMA((4 * TM + 1,)),
            pltpu.VMEM((TM, 128), jnp.int32),
        ],
        compiler_params=pltpu.CompilerParams(vmem_limit_bytes=VMEM_BYTES),
        cost_estimate=pl.CostEstimate(flops=10**10, bytes_accessed=10**7, transcendentals=10**7),
    )(*kv_parts, *q_parts)


def finish_kernel(levels_ref, home_ref, w_ref, gate_ref, out_ref, attn_ref):
    for group in range(GROUPS):
        base = 2 * BAND * (group // 2)
        if group % 2:
            places = (base + 4 * HD, base + 5 * HD, base + 3 * HD)
        else:
            places = (base, base + HD, base + 2 * HD)
        for head in range(3):
            at = HEAD_ROWS * head
            sizes, shrink = [], []
            for piece in range(PIECES):
                rows = home_ref[PIECES * group + piece, at + HD : at + HEAD_ROWS]
                size = None
                for digit in reversed(range(DIGITS)):
                    term = rows[digit : digit + 1] * 2.0 ** (DIGIT_BITS * (2 - digit))
                    size = term if size is None else size + term
                sizes.append(size)
                shrink.append(jnp.exp2(rows[DIGITS : DIGITS + 1] - HEAD_ROOM))
            best = sizes[0]
            for size in sizes[1:]:
                best = jnp.maximum(best, size)
            shares = [jnp.exp2(size - best) for size in sizes]
            norm = shares[0]
            for share in shares[1:]:
                norm = norm + share
            norm = 1.0 / norm
            acc = None
            for piece in range(PIECES):
                part = home_ref[PIECES * group + piece, at : at + HD] * (shares[piece] * norm * shrink[piece])
                acc = part if acc is None else acc + part
            attn_ref[places[head] : places[head] + HD] = acc.astype(BF16)
    mixed = lax.dot_general(
        attn_ref[...], w_ref[...], (((0,), (0,)), ((), ())), preferred_element_type=F32
    ) * gate_ref[...].reshape(1, D)
    for frame in range(FRAMES_DEV):
        rows = slice(SHARD * frame, SHARD * (frame + 1))
        limit = jnp.right_shift(jnp.int32(SHARD * 32), 2 * levels_ref[frame])
        used = lax.axis_index("seq") * SHARD < limit
        out_ref[rows] = jnp.where(used, mixed[rows], 0.0).astype(BF16)


def finish(frame_level, home, w_out, gate):
    vmem = pl.BlockSpec(memory_space=pltpu.VMEM)
    return pl.pallas_call(
        finish_kernel,
        out_shape=jax.ShapeDtypeStruct((ROWS, D), BF16),
        in_specs=[pl.BlockSpec(memory_space=pltpu.SMEM), vmem, vmem, vmem],
        out_specs=vmem,
        scratch_shapes=[pltpu.VMEM((H * HD, ROWS), BF16)],
        compiler_params=pltpu.CompilerParams(vmem_limit_bytes=VMEM_BYTES),
    )(frame_level, home, w_out, gate)


def permute(x, axis, to):
    return lax.ppermute(x, axis, [(i, to(i)) for i in range(lax.axis_size(axis))])


def other_core(i):
    return i ^ 1


def along_z(k):
    return lambda i: ((i >> 1) + k) % 4 * 2 + (i & 1)


def along_x(k):
    return lambda i: (i & ~3) | ((i + k) & 3)


def forward(i):
    return along_z(-1 if i & 1 else 1)(i)


def spread_frames(x, beside):
    below = permute(x, "tm", along_z(1))
    above = permute(x, "tm", along_z(-1))
    below, above, *beside = lax.optimization_barrier((below, above, *beside))
    core = lax.axis_index("tm") & 1
    far = permute(jnp.where(core == 0, below, above), "tm", forward)
    parts = []
    for one in (x, above, far, below):
        parts += [one, permute(one, "tm", other_core)]
    return parts, beside


def spread_queries(x):
    near = jnp.stack([x, permute(x, "seq", lambda i: i ^ 4)])
    return [near] + [permute(near, "seq", along_x(k)) for k in (1, 2, 3)]


def to_groups(x):
    return [x[0]] + [permute(x[k], "seq", lambda i, k=k: i ^ (8 * k)) for k in range(1, GROUPS)]


def per_device(tokens, mod_shift, mod_scale, out_gate, w_qkv, w_out, frame_time, frame_level):
    message = project(frame_time, frame_level, tokens.reshape(ROWS, D), mod_shift, mod_scale, w_qkv)
    parts = to_groups(message)
    kv_block = jnp.stack([part[:Q_AT] for part in parts])
    q_block = jnp.stack([part[Q_AT:] for part in parts])
    message = attend(*spread_frames(kv_block, spread_queries(q_block)))
    home = lax.all_to_all(message.astype(jnp.float16), "seq", split_axis=0, concat_axis=0, tiled=True)
    out = finish(frame_level, home.astype(F32), w_out, out_gate)
    return out.reshape(FRAMES_DEV, SHARD, D)


def solution(mesh):
    placed = (P("tm", "seq", None), P(), P(), P(), P(), P(), P("tm"), P("tm"))
    return jax.shard_map(
        per_device, mesh=mesh, in_specs=placed, out_specs=P("tm", "seq", None), check_vma=False
    )
```

```python
import math

import jax
import jax.numpy as jnp
from jax import lax
from jax.experimental import pallas as pl
from jax.experimental.pallas import tpu as pltpu
from jax.sharding import PartitionSpec as P

H = 12
HD = 64
GROUPS = 4
PIECES = 8
FRAMES_DEV = 4
SHARD = 32
ROWS = FRAMES_DEV * SHARD
D = 1536
TM = 8
FRAMES = TM * FRAMES_DEV
BAND = 3 * HD
WIDE = 4
DIGITS = 5
DIGIT_BITS = 11
LOWEST = -(2.0**33)
HEAD_ROOM = 13.0
KV_ROWS = 3 * ROWS
Q_ROWS = ROWS + ROWS // 2
NOTE_ROWS = 16
Q_AT = KV_ROWS + NOTE_ROWS
SUM_ROWS = 16
V_ROWS = HD + SUM_ROWS
EXCESS = 60.0
HEAD_ROWS = HD + 8
MSG_ROWS = 3 * HEAD_ROWS
CHUNKS_TILE = 8
KEY_TILE = CHUNKS_TILE * SHARD
QUERY_TILE = PIECES * SHARD
MAX_CHUNKS = FRAMES * GROUPS
MAX_TILES = MAX_CHUNKS // CHUNKS_TILE
SCALE = HD ** (-0.5) * math.log2(math.e)
TOP_START = -1e30
MASKED = -2e30
WIDE_VMEM = 56 * 1024 * 1024
VMEM_BYTES = 24 * 1024 * 1024
F32 = jnp.float32
BF16 = jnp.bfloat16


def lane_ids(shape):
    return lax.broadcasted_iota(jnp.int32, shape, len(shape) - 1)


def half_pair(left, right):
    return jnp.where(lane_ids(left.shape) < HD, left, right)


def project_kernel(
    times_ref, levels_ref, tokens_ref, shift_ref, scale_ref, wq_ref, wk_ref, wv_ref, kv_out, normed_ref
):
    step = pl.program_id(0)

    @pl.when(step == 0)
    def _():
        values = tokens_ref[...].astype(F32)
        center = jnp.mean(values, axis=-1, keepdims=True)
        spread = jnp.mean(jnp.square(values - center), axis=-1, keepdims=True)
        scaled = (values - center) * lax.rsqrt(spread + 1e-06)
        normed = scaled * (1.0 + scale_ref[...].reshape(1, D)) + shift_ref[...].reshape(1, D)
        normed_ref[...] = normed.astype(BF16)
        lane = lane_ids((NOTE_ROWS, 128))
        note = jnp.zeros((NOTE_ROWS, 128), jnp.int32)
        for frame in range(FRAMES_DEV):
            note = jnp.where(lane == frame, times_ref[frame], note)
            note = jnp.where(lane == FRAMES_DEV + frame, levels_ref[frame], note)
        for slot in range(GROUPS):
            kv_out[slot, KV_ROWS:Q_AT] = note.astype(F32).astype(BF16)

    normed = normed_ref[...]
    queries = jnp.dot(normed, wq_ref[...], preferred_element_type=F32)
    keys = jnp.dot(normed, wk_ref[...], preferred_element_type=F32)
    values = jnp.dot(normed, wv_ref[...], preferred_element_type=F32)
    mine = lax.axis_index("seq") // PIECES
    half = ROWS // 2
    for odd in range(2):
        slot = jnp.bitwise_xor(2 * step + odd, mine)
        pair = slice(256, 384) if odd else slice(0, 128)
        middle = slice(128, 256)
        key_mid, value_mid, query_mid = keys[:, middle], values[:, middle], queries[:, middle]
        if odd:
            third = half_pair(pltpu.roll(key_mid, HD, 1), value_mid)
            query_third = half_pair(pltpu.roll(query_mid[:half], HD, 1), query_mid[half:])
        else:
            third = half_pair(key_mid, pltpu.roll(value_mid, HD, 1))
            query_third = half_pair(query_mid[:half], pltpu.roll(query_mid[half:], HD, 1))
        kv_out[slot, :ROWS] = keys[:, pair].astype(BF16)
        kv_out[slot, ROWS : 2 * ROWS] = values[:, pair].astype(BF16)
        kv_out[slot, 2 * ROWS : KV_ROWS] = third.astype(BF16)
        kv_out[slot, Q_AT : Q_AT + ROWS] = queries[:, pair].astype(BF16)
        kv_out[slot, Q_AT + ROWS :] = query_third.astype(BF16)


def project(frame_time, frame_level, tokens, shift, scale, w_qkv):
    width = 2 * BAND
    whole = lambda *shape: pl.BlockSpec(shape, lambda j: (0,) * len(shape))
    smem = pl.BlockSpec(memory_space=pltpu.SMEM)
    return pl.pallas_call(
        project_kernel,
        out_shape=jax.ShapeDtypeStruct((GROUPS, Q_AT + Q_ROWS, 128), BF16),
        grid=(2,),
        in_specs=[
            smem,
            smem,
            whole(ROWS, D),
            whole(D),
            whole(D),
            pl.BlockSpec((D, width), lambda j: (0, j)),
            pl.BlockSpec((D, width), lambda j: (0, 2 + j)),
            pl.BlockSpec((D, width), lambda j: (0, 4 + j)),
        ],
        out_specs=whole(GROUPS, Q_AT + Q_ROWS, 128),
        scratch_shapes=[pltpu.VMEM((ROWS, D), BF16)],
        compiler_params=pltpu.CompilerParams(vmem_limit_bytes=WIDE_VMEM),
        cost_estimate=pl.CostEstimate(
            flops=2 * ROWS * D * 3 * H * HD, bytes_accessed=2 * D * 3 * H * HD, transcendentals=0
        ),
    )(frame_time, frame_level, tokens, shift, scale, w_qkv, w_qkv, w_qkv)


def attend_kernel(*refs):
    kv_parts, q_parts, out_ref = refs[:TM], refs[TM : TM + 4], refs[TM + 4]
    kv_buf, q_buf, packed, v_flip, q_ext, excess, note_buf, notes, slot_of, place, count_to, sems, notes_vmem = refs[TM + 5 :]
    seq = lax.axis_index("seq")
    group, piece = seq // PIECES, seq % PIECES
    y_low, x_at = piece // 4, piece % 4

    note_copies = [
        pltpu.make_async_copy(kv_parts[n].at[0, KV_ROWS:Q_AT], note_buf.at[n], sems.at[n]) for n in range(TM)
    ]
    kv_copies = [pltpu.make_async_copy(kv_parts[n], kv_buf.at[n], sems.at[TM + n]) for n in range(TM)]
    q_copies = []
    for n, part in enumerate(q_parts):
        from_x = jnp.bitwise_and(x_at - n, 3)
        for flip in range(2):
            to = 4 * jnp.bitwise_xor(y_low, flip) + from_x
            q_copies.append(pltpu.make_async_copy(part.at[flip], q_buf.at[to], sems.at[2 * TM + 2 * n + flip]))
    for copy in note_copies + kv_copies + q_copies:
        copy.start()
    for copy in note_copies:
        copy.wait()
    kept = [note_buf[n].astype(F32).astype(jnp.int32)[:1] for n in range(TM)]
    notes_vmem[...] = jnp.concatenate(kept, axis=0)
    to_scalars = pltpu.make_async_copy(notes_vmem, notes, sems.at[4 * TM])
    to_scalars.start()
    to_scalars.wait()

    def time_at(i):
        return notes[i // FRAMES_DEV, i % FRAMES_DEV]

    def level_at(i):
        return notes[i // FRAMES_DEV, FRAMES_DEV + i % FRAMES_DEV]

    def chunks_of(level):
        return jnp.where(level == 0, GROUPS, jnp.where((level == 1) | (piece < 2), 1, 0))

    for i in range(FRAMES):
        slot_of[time_at(i)] = i

    def lay_out(t, used):
        i = slot_of[t]
        place[i] = used
        used = used + chunks_of(level_at(i))
        count_to[i] = used
        return used

    total = lax.fori_loop(0, FRAMES, lay_out, 0)
    tiles = jnp.maximum((total + CHUNKS_TILE - 1) // CHUNKS_TILE, 1)
    wide = (tiles + WIDE - 1) // WIDE

    def clear(c, carry):
        packed[c] = jnp.zeros((3, SHARD, 128), BF16)
        return carry

    lax.fori_loop(total, wide * WIDE * CHUNKS_TILE, clear, 0)

    for slot in range(TM):
        kv_copies[slot].wait()
        for frame in range(FRAMES_DEV):
            i = slot * FRAMES_DEV + frame
            to, here = place[i], chunks_of(level_at(i))

            def move(a, slot=slot, frame=frame, to=to):
                for plane in range(3):
                    row = plane * ROWS + frame * SHARD
                    packed[to + a, plane] = kv_buf[slot, jnp.bitwise_xor(a, group), row : row + SHARD]

            @pl.when(here > 0)
            def _(move=move):
                move(0)

            @pl.when(here > 1)
            def _(move=move):
                for a in range(1, GROUPS):
                    move(a)

    eye = (
        lax.broadcasted_iota(jnp.int32, (128, 128), 0) == lax.broadcasted_iota(jnp.int32, (128, 128), 1)
    ).astype(BF16)
    flip_dims = (((1,), (1,)), ((), ()))

    def flip_values(w, largest):
        tile = packed.at[pl.ds(w * WIDE * CHUNKS_TILE, WIDE * CHUNKS_TILE)]
        pair = lax.dot_general(
            eye, tile[:, 1].reshape(WIDE * KEY_TILE, 128), flip_dims, preferred_element_type=F32
        )
        third = lax.dot_general(
            eye[HD:], tile[:, 2].reshape(WIDE * KEY_TILE, 128), flip_dims, preferred_element_type=F32
        )
        for head, rows in enumerate((pair[:HD], pair[HD:], third)):
            for n in range(WIDE):
                part = rows[:, n * KEY_TILE : (n + 1) * KEY_TILE]
                v_flip[w * WIDE + n, head, :HD] = part.astype(BF16)
                v_flip[w * WIDE + n, head, HD:] = jnp.ones((SUM_ROWS, KEY_TILE), BF16)
                largest = jnp.maximum(largest, jnp.abs(part))
        return largest

    largest = lax.fori_loop(0, wide, flip_values, jnp.zeros((HD, KEY_TILE), F32))
    largest = jnp.max(jnp.max(largest, axis=0, keepdims=True), axis=1, keepdims=True)
    power = jnp.clip(jnp.floor(jnp.log2(largest)), -100.0, 100.0)
    grow = jnp.exp2(HEAD_ROOM - power)
    for copy in q_copies:
        copy.wait()
    excess[...] = jnp.zeros((8, QUERY_TILE), F32)

    key_row = lax.broadcasted_iota(jnp.int32, (KEY_TILE, QUERY_TILE), 0)

    def score_tile(c, head, limit=None):
        k_tile = packed[pl.ds(c * CHUNKS_TILE, CHUNKS_TILE), 2 if head == 2 else 0].reshape(KEY_TILE, 128)
        scores = lax.dot_general(k_tile, q_ext[head], flip_dims, preferred_element_type=F32) * SCALE
        return scores if limit is None else jnp.where(key_row < limit, scores, MASKED)

    def weigh(c, head, weights):
        return jnp.dot(v_flip[c, head], weights.astype(BF16), preferred_element_type=F32)

    def tall_max(scores):
        return jnp.max(scores.reshape(KEY_TILE // 8, 8, QUERY_TILE), axis=0)

    def place_queries(a, frame):
        shards = q_buf.at[:, jnp.bitwise_xor(a, group)]
        pair = shards[:, SHARD * frame : SHARD * (frame + 1)].reshape(QUERY_TILE, 128).astype(F32)
        low = ROWS + SHARD * (frame % 2)
        third = shards[:, low : low + SHARD].reshape(QUERY_TILE, 128).astype(F32)
        if frame // 2:
            third = pltpu.roll(third, HD, 1)
        none = jnp.zeros_like(pair)
        q_ext[0] = half_pair(pair, none).astype(BF16)
        q_ext[1] = half_pair(none, pair).astype(BF16)
        q_ext[2] = half_pair(third, none).astype(BF16)

    def write(a, frame, head, top, acc):
        sums = acc[HD : HD + 1]
        some = sums > 0.0
        out = acc[:HD] * jnp.where(some, grow / sums, 0.0)
        rest = jnp.where(some, top + jnp.log2(sums), LOWEST)
        digits = []
        for digit in range(DIGITS):
            unit = 2.0 ** (DIGIT_BITS * (2 - digit))
            whole = jnp.floor(rest * (1.0 / unit) + 0.5)
            rest = rest - whole * unit
            digits.append(whole)
        digits += [jnp.broadcast_to(power, (1, QUERY_TILE))] + [jnp.zeros_like(rest)] * 2
        rows = jnp.concatenate([out] + digits, axis=0)
        lanes = slice(SHARD * frame, SHARD * (frame + 1))
        for part in range(QUERY_TILE // 128):
            block = rows[:, 128 * part : 128 * (part + 1)]
            for sub in range(128 // SHARD):
                shift = (SHARD * (frame - sub)) % 128
                turned = pltpu.roll(block, shift, 1) if shift else block
                home = PIECES * a + 128 // SHARD * part + sub
                out_ref[home, HEAD_ROWS * head : HEAD_ROWS * (head + 1), lanes] = turned[:, lanes]

    def plan(frame):
        query_tiles = jnp.where(level_at(frame) == 0, GROUPS, 1)
        chunks = count_to[frame]
        key_tiles = jnp.maximum((chunks + CHUNKS_TILE - 1) // CHUNKS_TILE, 1)
        return query_tiles, key_tiles, (chunks - (key_tiles - 1) * CHUNKS_TILE) * SHARD

    for frame in range(FRAMES_DEV):
        query_tiles, key_tiles, last_rows = plan(frame)

        def one_query_tile(a, carry, frame=frame, key_tiles=key_tiles, last_rows=last_rows):
            place_queries(a, frame)
            full = key_tiles - 1
            first = [score_tile(full, head, last_rows) for head in range(3)]
            tops = [jnp.maximum(jnp.max(scores, axis=0, keepdims=True), TOP_START) for scores in first]
            first = [jnp.exp2(scores - top) for scores, top in zip(first, tops)]
            state = []
            for head in range(3):
                state.append(weigh(full, head, first[head]))
                state.append(jnp.broadcast_to(tops[head], (8, QUERY_TILE)))

            def key_steps(count):
                def run(c, state):
                    state = list(state)
                    items = [(count * c + n, head) for n in range(count) for head in range(3)]
                    scores = [score_tile(tile, head) for tile, head in items]
                    weights = [
                        jnp.exp2(one - tops[head]).astype(BF16) for one, (_, head) in zip(scores, items)
                    ]
                    for (tile, head), one, weight in zip(items, scores, weights):
                        state[2 * head] = state[2 * head] + weigh(tile, head, weight)
                        state[2 * head + 1] = jnp.maximum(state[2 * head + 1], tall_max(one))
                    return tuple(state)

                return run

            state = lax.fori_loop(0, full // 2, key_steps(2), tuple(state))
            state = lax.fori_loop(full // 2 * 2, full, key_steps(1), state)
            over = excess[...]
            for head in range(3):
                write(a, frame, head, tops[head], state[2 * head])
                over = jnp.maximum(over, state[2 * head + 1] - tops[head])
            excess[...] = over
            return carry

        lax.fori_loop(0, query_tiles, one_query_tile, 0)

    @pl.when(jnp.max(excess[...]) > EXCESS)
    def _():
        for frame in range(FRAMES_DEV):
            query_tiles, key_tiles, last_rows = plan(frame)

            def redo(a, carry, frame=frame, key_tiles=key_tiles, last_rows=last_rows):
                place_queries(a, frame)
                for head in range(3):

                    def one_key_tile(c, state, head=head):
                        top, acc = state
                        scores = score_tile(c, head, jnp.where(c == key_tiles - 1, last_rows, KEY_TILE))
                        new_top = jnp.maximum(top, jnp.max(scores, axis=0, keepdims=True))
                        acc = acc * jnp.exp2(top - new_top) + weigh(c, head, jnp.exp2(scores - new_top))
                        return new_top, acc

                    start = (jnp.full((1, QUERY_TILE), TOP_START, F32), jnp.zeros((V_ROWS, QUERY_TILE), F32))
                    top, acc = lax.fori_loop(0, key_tiles, one_key_tile, start)
                    write(a, frame, head, top, acc)
                return carry

            lax.fori_loop(0, query_tiles, redo, 0)


def attend(kv_parts, q_parts):
    hbm = pl.BlockSpec(memory_space=pl.ANY)
    vmem = pl.BlockSpec(memory_space=pltpu.VMEM)
    return pl.pallas_call(
        attend_kernel,
        out_shape=jax.ShapeDtypeStruct((32, MSG_ROWS, 128), F32),
        in_specs=[hbm] * (TM + 4),
        out_specs=vmem,
        scratch_shapes=[
            pltpu.VMEM((TM, GROUPS, Q_AT, 128), BF16),
            pltpu.VMEM((PIECES, GROUPS, Q_ROWS, 128), BF16),
            pltpu.VMEM((MAX_CHUNKS, 3, SHARD, 128), BF16),
            pltpu.VMEM((MAX_TILES, 3, V_ROWS, KEY_TILE), BF16),
            pltpu.VMEM((3, QUERY_TILE, 128), BF16),
            pltpu.VMEM((8, QUERY_TILE), F32),
            pltpu.VMEM((TM, NOTE_ROWS, 128), BF16),
            pltpu.SMEM((TM, 128), jnp.int32),
            pltpu.SMEM((FRAMES,), jnp.int32),
            pltpu.SMEM((FRAMES,), jnp.int32),
            pltpu.SMEM((FRAMES,), jnp.int32),
            pltpu.SemaphoreType.DMA((4 * TM + 1,)),
            pltpu.VMEM((TM, 128), jnp.int32),
        ],
        compiler_params=pltpu.CompilerParams(vmem_limit_bytes=VMEM_BYTES),
        cost_estimate=pl.CostEstimate(flops=10**10, bytes_accessed=10**7, transcendentals=10**7),
    )(*kv_parts, *q_parts)


def finish_kernel(levels_ref, home_ref, w_ref, gate_ref, out_ref, attn_ref):
    for group in range(GROUPS):
        base = 2 * BAND * (group // 2)
        if group % 2:
            places = (base + 4 * HD, base + 5 * HD, base + 3 * HD)
        else:
            places = (base, base + HD, base + 2 * HD)
        for head in range(3):
            at = HEAD_ROWS * head
            sizes, shrink = [], []
            for piece in range(PIECES):
                rows = home_ref[PIECES * group + piece, at + HD : at + HEAD_ROWS]
                size = None
                for digit in reversed(range(DIGITS)):
                    term = rows[digit : digit + 1] * 2.0 ** (DIGIT_BITS * (2 - digit))
                    size = term if size is None else size + term
                sizes.append(size)
                shrink.append(jnp.exp2(rows[DIGITS : DIGITS + 1] - HEAD_ROOM))
            best = sizes[0]
            for size in sizes[1:]:
                best = jnp.maximum(best, size)
            shares = [jnp.exp2(size - best) for size in sizes]
            norm = shares[0]
            for share in shares[1:]:
                norm = norm + share
            norm = 1.0 / norm
            acc = None
            for piece in range(PIECES):
                part = home_ref[PIECES * group + piece, at : at + HD] * (shares[piece] * norm * shrink[piece])
                acc = part if acc is None else acc + part
            attn_ref[places[head] : places[head] + HD] = acc.astype(BF16)
    mixed = lax.dot_general(
        attn_ref[...], w_ref[...], (((0,), (0,)), ((), ())), preferred_element_type=F32
    ) * gate_ref[...].reshape(1, D)
    for frame in range(FRAMES_DEV):
        rows = slice(SHARD * frame, SHARD * (frame + 1))
        limit = jnp.right_shift(jnp.int32(SHARD * 32), 2 * levels_ref[frame])
        used = lax.axis_index("seq") * SHARD < limit
        out_ref[rows] = jnp.where(used, mixed[rows], 0.0).astype(BF16)


def finish(frame_level, home, w_out, gate):
    vmem = pl.BlockSpec(memory_space=pltpu.VMEM)
    return pl.pallas_call(
        finish_kernel,
        out_shape=jax.ShapeDtypeStruct((ROWS, D), BF16),
        in_specs=[pl.BlockSpec(memory_space=pltpu.SMEM), vmem, vmem, vmem],
        out_specs=vmem,
        scratch_shapes=[pltpu.VMEM((H * HD, ROWS), BF16)],
        compiler_params=pltpu.CompilerParams(vmem_limit_bytes=VMEM_BYTES),
    )(frame_level, home, w_out, gate)


def permute(x, axis, to):
    return lax.ppermute(x, axis, [(i, to(i)) for i in range(lax.axis_size(axis))])


def other_core(i):
    return i ^ 1


def along_z(k):
    return lambda i: ((i >> 1) + k) % 4 * 2 + (i & 1)


def along_x(k):
    return lambda i: (i & ~3) | ((i + k) & 3)


def forward(i):
    return along_z(-1 if i & 1 else 1)(i)


def spread_frames(x, beside):
    below = permute(x, "tm", along_z(1))
    above = permute(x, "tm", along_z(-1))
    below, above, *beside = lax.optimization_barrier((below, above, *beside))
    core = lax.axis_index("tm") & 1
    far = permute(jnp.where(core == 0, below, above), "tm", forward)
    parts = []
    for one in (x, above, far, below):
        parts += [one, permute(one, "tm", other_core)]
    return parts, beside


def spread_queries(x):
    near = jnp.stack([x, permute(x, "seq", lambda i: i ^ 4)])
    return [near] + [permute(near, "seq", along_x(k)) for k in (1, 2, 3)]


def to_groups(x):
    return [x[0]] + [permute(x[k], "seq", lambda i, k=k: i ^ (8 * k)) for k in range(1, GROUPS)]


def per_device(tokens, mod_shift, mod_scale, out_gate, w_qkv, w_out, frame_time, frame_level):
    message = project(frame_time, frame_level, tokens.reshape(ROWS, D), mod_shift, mod_scale, w_qkv)
    parts = to_groups(message)
    kv_block = jnp.stack([part[:Q_AT] for part in parts])
    q_block = jnp.stack([part[Q_AT:] for part in parts])
    message = attend(*spread_frames(kv_block, spread_queries(q_block)))
    home = lax.all_to_all(message.astype(jnp.float16), "seq", split_axis=0, concat_axis=0, tiled=True)
    out = finish(frame_level, home.astype(F32), w_out, out_gate)
    return out.reshape(FRAMES_DEV, SHARD, D)


def solution(mesh):
    placed = (P("tm", "seq", None), P(), P(), P(), P(), P(), P("tm"), P("tm"))
    return jax.shard_map(
        per_device, mesh=mesh, in_specs=placed, out_specs=P("tm", "seq", None), check_vma=False
    )
```

```python
import math

import jax
import jax.numpy as jnp
from jax import lax
from jax.experimental import pallas as pl
from jax.experimental.pallas import tpu as pltpu
from jax.sharding import PartitionSpec as P

H = 12
HD = 64
GROUPS = 4
PIECES = 8
FRAMES_DEV = 4
SHARD = 32
ROWS = FRAMES_DEV * SHARD
D = 1536
TM = 8
FRAMES = TM * FRAMES_DEV
BAND = 3 * HD
WIDE = 4
DIGITS = 5
DIGIT_BITS = 11
LOWEST = -(2.0**33)
HEAD_ROOM = 13.0
KV_ROWS = 3 * ROWS
Q_ROWS = ROWS + ROWS // 2
NOTE_ROWS = 16
Q_AT = KV_ROWS + NOTE_ROWS
SUM_ROWS = 16
V_ROWS = HD + SUM_ROWS
EXCESS = 60.0
HEAD_ROWS = HD + 8
MSG_ROWS = 3 * HEAD_ROWS
CHUNKS_TILE = 8
KEY_TILE = CHUNKS_TILE * SHARD
QUERY_TILE = PIECES * SHARD
MAX_CHUNKS = FRAMES * GROUPS
MAX_TILES = MAX_CHUNKS // CHUNKS_TILE
SCALE = HD ** (-0.5) * math.log2(math.e)
TOP_START = -1e30
MASKED = -2e30
WIDE_VMEM = 56 * 1024 * 1024
VMEM_BYTES = 24 * 1024 * 1024
F32 = jnp.float32
BF16 = jnp.bfloat16


def lane_ids(shape):
    return lax.broadcasted_iota(jnp.int32, shape, len(shape) - 1)


def half_pair(left, right):
    return jnp.where(lane_ids(left.shape) < HD, left, right)


def project_kernel(
    times_ref, levels_ref, tokens_ref, shift_ref, scale_ref, wq_ref, wk_ref, wv_ref, kv_out, normed_ref
):
    step = pl.program_id(0)

    @pl.when(step == 0)
    def _():
        values = tokens_ref[...].astype(F32)
        center = jnp.mean(values, axis=-1, keepdims=True)
        spread = jnp.mean(jnp.square(values - center), axis=-1, keepdims=True)
        scaled = (values - center) * lax.rsqrt(spread + 1e-06)
        normed = scaled * (1.0 + scale_ref[...].reshape(1, D)) + shift_ref[...].reshape(1, D)
        normed_ref[...] = normed.astype(BF16)
        lane = lane_ids((NOTE_ROWS, 128))
        note = jnp.zeros((NOTE_ROWS, 128), jnp.int32)
        for frame in range(FRAMES_DEV):
            note = jnp.where(lane == frame, times_ref[frame], note)
            note = jnp.where(lane == FRAMES_DEV + frame, levels_ref[frame], note)
        for slot in range(GROUPS):
            kv_out[slot, KV_ROWS:Q_AT] = note.astype(F32).astype(BF16)

    normed = normed_ref[...]
    queries = jnp.dot(normed, wq_ref[...], preferred_element_type=F32)
    keys = jnp.dot(normed, wk_ref[...], preferred_element_type=F32)
    values = jnp.dot(normed, wv_ref[...], preferred_element_type=F32)
    mine = lax.axis_index("seq") // PIECES
    half = ROWS // 2
    for odd in range(2):
        slot = jnp.bitwise_xor(2 * step + odd, mine)
        pair = slice(256, 384) if odd else slice(0, 128)
        middle = slice(128, 256)
        key_mid, value_mid, query_mid = keys[:, middle], values[:, middle], queries[:, middle]
        if odd:
            third = half_pair(pltpu.roll(key_mid, HD, 1), value_mid)
            query_third = half_pair(pltpu.roll(query_mid[:half], HD, 1), query_mid[half:])
        else:
            third = half_pair(key_mid, pltpu.roll(value_mid, HD, 1))
            query_third = half_pair(query_mid[:half], pltpu.roll(query_mid[half:], HD, 1))
        kv_out[slot, :ROWS] = keys[:, pair].astype(BF16)
        kv_out[slot, ROWS : 2 * ROWS] = values[:, pair].astype(BF16)
        kv_out[slot, 2 * ROWS : KV_ROWS] = third.astype(BF16)
        kv_out[slot, Q_AT : Q_AT + ROWS] = queries[:, pair].astype(BF16)
        kv_out[slot, Q_AT + ROWS :] = query_third.astype(BF16)


def project(frame_time, frame_level, tokens, shift, scale, w_qkv):
    width = 2 * BAND
    whole = lambda *shape: pl.BlockSpec(shape, lambda j: (0,) * len(shape))
    smem = pl.BlockSpec(memory_space=pltpu.SMEM)
    return pl.pallas_call(
        project_kernel,
        out_shape=jax.ShapeDtypeStruct((GROUPS, Q_AT + Q_ROWS, 128), BF16),
        grid=(2,),
        in_specs=[
            smem,
            smem,
            whole(ROWS, D),
            whole(D),
            whole(D),
            pl.BlockSpec((D, width), lambda j: (0, j)),
            pl.BlockSpec((D, width), lambda j: (0, 2 + j)),
            pl.BlockSpec((D, width), lambda j: (0, 4 + j)),
        ],
        out_specs=whole(GROUPS, Q_AT + Q_ROWS, 128),
        scratch_shapes=[pltpu.VMEM((ROWS, D), BF16)],
        compiler_params=pltpu.CompilerParams(vmem_limit_bytes=WIDE_VMEM),
        cost_estimate=pl.CostEstimate(
            flops=2 * ROWS * D * 3 * H * HD, bytes_accessed=2 * D * 3 * H * HD, transcendentals=0
        ),
    )(frame_time, frame_level, tokens, shift, scale, w_qkv, w_qkv, w_qkv)


def attend_kernel(*refs):
    kv_parts, q_parts, out_ref = refs[:TM], refs[TM : TM + 4], refs[TM + 4]
    kv_buf, q_buf, packed, v_flip, q_ext, excess, note_buf, notes, slot_of, place, count_to, sems, notes_vmem = refs[TM + 5 :]
    seq = lax.axis_index("seq")
    group, piece = seq // PIECES, seq % PIECES
    y_low, x_at = piece // 4, piece % 4

    note_copies = [
        pltpu.make_async_copy(kv_parts[n].at[0, KV_ROWS:Q_AT], note_buf.at[n], sems.at[n]) for n in range(TM)
    ]
    kv_copies = [pltpu.make_async_copy(kv_parts[n], kv_buf.at[n], sems.at[TM + n]) for n in range(TM)]
    q_copies = []
    for n, part in enumerate(q_parts):
        from_x = jnp.bitwise_and(x_at - n, 3)
        for flip in range(2):
            to = 4 * jnp.bitwise_xor(y_low, flip) + from_x
            q_copies.append(pltpu.make_async_copy(part.at[flip], q_buf.at[to], sems.at[2 * TM + 2 * n + flip]))
    for copy in note_copies + kv_copies + q_copies:
        copy.start()
    for copy in note_copies:
        copy.wait()
    kept = [note_buf[n].astype(F32).astype(jnp.int32)[:1] for n in range(TM)]
    notes_vmem[...] = jnp.concatenate(kept, axis=0)
    to_scalars = pltpu.make_async_copy(notes_vmem, notes, sems.at[4 * TM])
    to_scalars.start()
    to_scalars.wait()

    def time_at(i):
        return notes[i // FRAMES_DEV, i % FRAMES_DEV]

    def level_at(i):
        return notes[i // FRAMES_DEV, FRAMES_DEV + i % FRAMES_DEV]

    def chunks_of(level):
        return jnp.where(level == 0, GROUPS, jnp.where((level == 1) | (piece < 2), 1, 0))

    for i in range(FRAMES):
        slot_of[time_at(i)] = i

    def lay_out(t, used):
        i = slot_of[t]
        place[i] = used
        used = used + chunks_of(level_at(i))
        count_to[i] = used
        return used

    total = lax.fori_loop(0, FRAMES, lay_out, 0)
    tiles = jnp.maximum((total + CHUNKS_TILE - 1) // CHUNKS_TILE, 1)
    wide = (tiles + WIDE - 1) // WIDE

    def clear(c, carry):
        packed[c] = jnp.zeros((3, SHARD, 128), BF16)
        return carry

    lax.fori_loop(total, wide * WIDE * CHUNKS_TILE, clear, 0)

    for slot in range(TM):
        kv_copies[slot].wait()
        for frame in range(FRAMES_DEV):
            i = slot * FRAMES_DEV + frame
            to, here = place[i], chunks_of(level_at(i))

            def move(a, slot=slot, frame=frame, to=to):
                for plane in range(3):
                    row = plane * ROWS + frame * SHARD
                    packed[to + a, plane] = kv_buf[slot, jnp.bitwise_xor(a, group), row : row + SHARD]

            @pl.when(here > 0)
            def _(move=move):
                move(0)

            @pl.when(here > 1)
            def _(move=move):
                for a in range(1, GROUPS):
                    move(a)

    eye = (
        lax.broadcasted_iota(jnp.int32, (128, 128), 0) == lax.broadcasted_iota(jnp.int32, (128, 128), 1)
    ).astype(BF16)
    flip_dims = (((1,), (1,)), ((), ()))

    def flip_values(w, largest):
        tile = packed.at[pl.ds(w * WIDE * CHUNKS_TILE, WIDE * CHUNKS_TILE)]
        pair = lax.dot_general(
            eye, tile[:, 1].reshape(WIDE * KEY_TILE, 128), flip_dims, preferred_element_type=F32
        )
        third = lax.dot_general(
            eye[HD:], tile[:, 2].reshape(WIDE * KEY_TILE, 128), flip_dims, preferred_element_type=F32
        )
        for head, rows in enumerate((pair[:HD], pair[HD:], third)):
            for n in range(WIDE):
                part = rows[:, n * KEY_TILE : (n + 1) * KEY_TILE]
                v_flip[w * WIDE + n, head, :HD] = part.astype(BF16)
                v_flip[w * WIDE + n, head, HD:] = jnp.ones((SUM_ROWS, KEY_TILE), BF16)
                largest = jnp.maximum(largest, jnp.abs(part))
        return largest

    largest = lax.fori_loop(0, wide, flip_values, jnp.zeros((HD, KEY_TILE), F32))
    largest = jnp.max(jnp.max(largest, axis=0, keepdims=True), axis=1, keepdims=True)
    power = jnp.clip(jnp.floor(jnp.log2(largest)), -100.0, 100.0)
    grow = jnp.exp2(HEAD_ROOM - power)
    for copy in q_copies:
        copy.wait()
    excess[...] = jnp.zeros((8, QUERY_TILE), F32)

    key_row = lax.broadcasted_iota(jnp.int32, (KEY_TILE, QUERY_TILE), 0)

    def score_tile(c, head, limit=None):
        k_tile = packed[pl.ds(c * CHUNKS_TILE, CHUNKS_TILE), 2 if head == 2 else 0].reshape(KEY_TILE, 128)
        scores = lax.dot_general(k_tile, q_ext[head], flip_dims, preferred_element_type=F32) * SCALE
        return scores if limit is None else jnp.where(key_row < limit, scores, MASKED)

    def weigh(c, head, weights):
        return jnp.dot(v_flip[c, head], weights.astype(BF16), preferred_element_type=F32)

    def tall_max(scores):
        return jnp.max(scores.reshape(KEY_TILE // 8, 8, QUERY_TILE), axis=0)

    def place_queries(a, frame):
        shards = q_buf.at[:, jnp.bitwise_xor(a, group)]
        pair = shards[:, SHARD * frame : SHARD * (frame + 1)].reshape(QUERY_TILE, 128).astype(F32)
        low = ROWS + SHARD * (frame % 2)
        third = shards[:, low : low + SHARD].reshape(QUERY_TILE, 128).astype(F32)
        if frame // 2:
            third = pltpu.roll(third, HD, 1)
        none = jnp.zeros_like(pair)
        q_ext[0] = half_pair(pair, none).astype(BF16)
        q_ext[1] = half_pair(none, pair).astype(BF16)
        q_ext[2] = half_pair(third, none).astype(BF16)

    def write(a, frame, head, top, acc):
        sums = acc[HD : HD + 1]
        some = sums > 0.0
        out = acc[:HD] * jnp.where(some, grow / sums, 0.0)
        rest = jnp.where(some, top + jnp.log2(sums), LOWEST)
        digits = []
        for digit in range(DIGITS):
            unit = 2.0 ** (DIGIT_BITS * (2 - digit))
            whole = jnp.floor(rest * (1.0 / unit) + 0.5)
            rest = rest - whole * unit
            digits.append(whole)
        digits += [jnp.broadcast_to(power, (1, QUERY_TILE))] + [jnp.zeros_like(rest)] * 2
        rows = jnp.concatenate([out] + digits, axis=0)
        lanes = slice(SHARD * frame, SHARD * (frame + 1))
        for part in range(QUERY_TILE // 128):
            block = rows[:, 128 * part : 128 * (part + 1)]
            for sub in range(128 // SHARD):
                shift = (SHARD * (frame - sub)) % 128
                turned = pltpu.roll(block, shift, 1) if shift else block
                home = PIECES * a + 128 // SHARD * part + sub
                out_ref[home, HEAD_ROWS * head : HEAD_ROWS * (head + 1), lanes] = turned[:, lanes]

    def plan(frame):
        query_tiles = jnp.where(level_at(frame) == 0, GROUPS, 1)
        chunks = count_to[frame]
        key_tiles = jnp.maximum((chunks + CHUNKS_TILE - 1) // CHUNKS_TILE, 1)
        return query_tiles, key_tiles, (chunks - (key_tiles - 1) * CHUNKS_TILE) * SHARD

    for frame in range(FRAMES_DEV):
        query_tiles, key_tiles, last_rows = plan(frame)

        def one_query_tile(a, carry, frame=frame, key_tiles=key_tiles, last_rows=last_rows):
            place_queries(a, frame)
            full = key_tiles - 1
            first = [score_tile(full, head, last_rows) for head in range(3)]
            tops = [jnp.maximum(jnp.max(scores, axis=0, keepdims=True), TOP_START) for scores in first]
            first = [jnp.exp2(scores - top) for scores, top in zip(first, tops)]
            state = []
            for head in range(3):
                state.append(weigh(full, head, first[head]))
                state.append(jnp.broadcast_to(tops[head], (8, QUERY_TILE)))

            def key_steps(count):
                def run(c, state):
                    state = list(state)
                    items = [(count * c + n, head) for n in range(count) for head in range(3)]
                    scores = [score_tile(tile, head) for tile, head in items]
                    weights = [
                        jnp.exp2(one - tops[head]).astype(BF16) for one, (_, head) in zip(scores, items)
                    ]
                    for (tile, head), one, weight in zip(items, scores, weights):
                        state[2 * head] = state[2 * head] + weigh(tile, head, weight)
                        state[2 * head + 1] = jnp.maximum(state[2 * head + 1], tall_max(one))
                    return tuple(state)

                return run

            state = lax.fori_loop(0, full // 4, key_steps(4), tuple(state))
            state = lax.fori_loop(full // 4 * 2, full // 2, key_steps(2), state)
            state = lax.fori_loop(full // 2 * 2, full, key_steps(1), state)
            over = excess[...]
            for head in range(3):
                write(a, frame, head, tops[head], state[2 * head])
                over = jnp.maximum(over, state[2 * head + 1] - tops[head])
            excess[...] = over
            return carry

        lax.fori_loop(0, query_tiles, one_query_tile, 0)

    @pl.when(jnp.max(excess[...]) > EXCESS)
    def _():
        for frame in range(FRAMES_DEV):
            query_tiles, key_tiles, last_rows = plan(frame)

            def redo(a, carry, frame=frame, key_tiles=key_tiles, last_rows=last_rows):
                place_queries(a, frame)
                for head in range(3):

                    def one_key_tile(c, state, head=head):
                        top, acc = state
                        scores = score_tile(c, head, jnp.where(c == key_tiles - 1, last_rows, KEY_TILE))
                        new_top = jnp.maximum(top, jnp.max(scores, axis=0, keepdims=True))
                        acc = acc * jnp.exp2(top - new_top) + weigh(c, head, jnp.exp2(scores - new_top))
                        return new_top, acc

                    start = (jnp.full((1, QUERY_TILE), TOP_START, F32), jnp.zeros((V_ROWS, QUERY_TILE), F32))
                    top, acc = lax.fori_loop(0, key_tiles, one_key_tile, start)
                    write(a, frame, head, top, acc)
                return carry

            lax.fori_loop(0, query_tiles, redo, 0)


def attend(kv_parts, q_parts):
    hbm = pl.BlockSpec(memory_space=pl.ANY)
    vmem = pl.BlockSpec(memory_space=pltpu.VMEM)
    return pl.pallas_call(
        attend_kernel,
        out_shape=jax.ShapeDtypeStruct((32, MSG_ROWS, 128), F32),
        in_specs=[hbm] * (TM + 4),
        out_specs=vmem,
        scratch_shapes=[
            pltpu.VMEM((TM, GROUPS, Q_AT, 128), BF16),
            pltpu.VMEM((PIECES, GROUPS, Q_ROWS, 128), BF16),
            pltpu.VMEM((MAX_CHUNKS, 3, SHARD, 128), BF16),
            pltpu.VMEM((MAX_TILES, 3, V_ROWS, KEY_TILE), BF16),
            pltpu.VMEM((3, QUERY_TILE, 128), BF16),
            pltpu.VMEM((8, QUERY_TILE), F32),
            pltpu.VMEM((TM, NOTE_ROWS, 128), BF16),
            pltpu.SMEM((TM, 128), jnp.int32),
            pltpu.SMEM((FRAMES,), jnp.int32),
            pltpu.SMEM((FRAMES,), jnp.int32),
            pltpu.SMEM((FRAMES,), jnp.int32),
            pltpu.SemaphoreType.DMA((4 * TM + 1,)),
            pltpu.VMEM((TM, 128), jnp.int32),
        ],
        compiler_params=pltpu.CompilerParams(vmem_limit_bytes=VMEM_BYTES),
        cost_estimate=pl.CostEstimate(flops=10**10, bytes_accessed=10**7, transcendentals=10**7),
    )(*kv_parts, *q_parts)


def finish_kernel(levels_ref, home_ref, w_ref, gate_ref, out_ref, attn_ref):
    for group in range(GROUPS):
        base = 2 * BAND * (group // 2)
        if group % 2:
            places = (base + 4 * HD, base + 5 * HD, base + 3 * HD)
        else:
            places = (base, base + HD, base + 2 * HD)
        for head in range(3):
            at = HEAD_ROWS * head
            sizes, shrink = [], []
            for piece in range(PIECES):
                rows = home_ref[PIECES * group + piece, at + HD : at + HEAD_ROWS]
                size = None
                for digit in reversed(range(DIGITS)):
                    term = rows[digit : digit + 1] * 2.0 ** (DIGIT_BITS * (2 - digit))
                    size = term if size is None else size + term
                sizes.append(size)
                shrink.append(jnp.exp2(rows[DIGITS : DIGITS + 1] - HEAD_ROOM))
            best = sizes[0]
            for size in sizes[1:]:
                best = jnp.maximum(best, size)
            shares = [jnp.exp2(size - best) for size in sizes]
            norm = shares[0]
            for share in shares[1:]:
                norm = norm + share
            norm = 1.0 / norm
            acc = None
            for piece in range(PIECES):
                part = home_ref[PIECES * group + piece, at : at + HD] * (shares[piece] * norm * shrink[piece])
                acc = part if acc is None else acc + part
            attn_ref[places[head] : places[head] + HD] = acc.astype(BF16)
    mixed = lax.dot_general(
        attn_ref[...], w_ref[...], (((0,), (0,)), ((), ())), preferred_element_type=F32
    ) * gate_ref[...].reshape(1, D)
    for frame in range(FRAMES_DEV):
        rows = slice(SHARD * frame, SHARD * (frame + 1))
        limit = jnp.right_shift(jnp.int32(SHARD * 32), 2 * levels_ref[frame])
        used = lax.axis_index("seq") * SHARD < limit
        out_ref[rows] = jnp.where(used, mixed[rows], 0.0).astype(BF16)


def finish(frame_level, home, w_out, gate):
    vmem = pl.BlockSpec(memory_space=pltpu.VMEM)
    return pl.pallas_call(
        finish_kernel,
        out_shape=jax.ShapeDtypeStruct((ROWS, D), BF16),
        in_specs=[pl.BlockSpec(memory_space=pltpu.SMEM), vmem, vmem, vmem],
        out_specs=vmem,
        scratch_shapes=[pltpu.VMEM((H * HD, ROWS), BF16)],
        compiler_params=pltpu.CompilerParams(vmem_limit_bytes=VMEM_BYTES),
    )(frame_level, home, w_out, gate)


def permute(x, axis, to):
    return lax.ppermute(x, axis, [(i, to(i)) for i in range(lax.axis_size(axis))])


def other_core(i):
    return i ^ 1


def along_z(k):
    return lambda i: ((i >> 1) + k) % 4 * 2 + (i & 1)


def along_x(k):
    return lambda i: (i & ~3) | ((i + k) & 3)


def forward(i):
    return along_z(-1 if i & 1 else 1)(i)


def spread_frames(x, beside):
    below = permute(x, "tm", along_z(1))
    above = permute(x, "tm", along_z(-1))
    below, above, *beside = lax.optimization_barrier((below, above, *beside))
    core = lax.axis_index("tm") & 1
    far = permute(jnp.where(core == 0, below, above), "tm", forward)
    parts = []
    for one in (x, above, far, below):
        parts += [one, permute(one, "tm", other_core)]
    return parts, beside


def spread_queries(x):
    near = jnp.stack([x, permute(x, "seq", lambda i: i ^ 4)])
    return [near] + [permute(near, "seq", along_x(k)) for k in (1, 2, 3)]


def to_groups(x):
    return [x[0]] + [permute(x[k], "seq", lambda i, k=k: i ^ (8 * k)) for k in range(1, GROUPS)]


def per_device(tokens, mod_shift, mod_scale, out_gate, w_qkv, w_out, frame_time, frame_level):
    message = project(frame_time, frame_level, tokens.reshape(ROWS, D), mod_shift, mod_scale, w_qkv)
    parts = to_groups(message)
    kv_block = jnp.stack([part[:Q_AT] for part in parts])
    q_block = jnp.stack([part[Q_AT:] for part in parts])
    message = attend(*spread_frames(kv_block, spread_queries(q_block)))
    home = lax.all_to_all(message.astype(jnp.float16), "seq", split_axis=0, concat_axis=0, tiled=True)
    out = finish(frame_level, home.astype(F32), w_out, out_gate)
    return out.reshape(FRAMES_DEV, SHARD, D)


def solution(mesh):
    placed = (P("tm", "seq", None), P(), P(), P(), P(), P(), P("tm"), P("tm"))
    return jax.shard_map(
        per_device, mesh=mesh, in_specs=placed, out_specs=P("tm", "seq", None), check_vma=False
    )
```

```python
import math

import jax
import jax.numpy as jnp
from jax import lax
from jax.experimental import pallas as pl
from jax.experimental.pallas import tpu as pltpu
from jax.sharding import PartitionSpec as P

H = 12
HD = 64
GROUPS = 4
PIECES = 8
FRAMES_DEV = 4
SHARD = 32
ROWS = FRAMES_DEV * SHARD
D = 1536
TM = 8
FRAMES = TM * FRAMES_DEV
BAND = 3 * HD
WIDE = 8
DIGITS = 5
DIGIT_BITS = 11
LOWEST = -(2.0**33)
HEAD_ROOM = 13.0
KV_ROWS = 3 * ROWS
Q_ROWS = ROWS + ROWS // 2
NOTE_ROWS = 16
Q_AT = KV_ROWS + NOTE_ROWS
SUM_ROWS = 16
V_ROWS = HD + SUM_ROWS
EXCESS = 60.0
HEAD_ROWS = HD + 8
MSG_ROWS = 3 * HEAD_ROWS
CHUNKS_TILE = 8
KEY_TILE = CHUNKS_TILE * SHARD
QUERY_TILE = PIECES * SHARD
MAX_CHUNKS = FRAMES * GROUPS
MAX_TILES = MAX_CHUNKS // CHUNKS_TILE
SCALE = HD ** (-0.5) * math.log2(math.e)
TOP_START = -1e30
MASKED = -2e30
WIDE_VMEM = 56 * 1024 * 1024
VMEM_BYTES = 24 * 1024 * 1024
F32 = jnp.float32
BF16 = jnp.bfloat16


def lane_ids(shape):
    return lax.broadcasted_iota(jnp.int32, shape, len(shape) - 1)


def half_pair(left, right):
    return jnp.where(lane_ids(left.shape) < HD, left, right)


def project_kernel(
    times_ref, levels_ref, tokens_ref, shift_ref, scale_ref, wq_ref, wk_ref, wv_ref, kv_out, normed_ref
):
    step = pl.program_id(0)

    @pl.when(step == 0)
    def _():
        values = tokens_ref[...].astype(F32)
        center = jnp.mean(values, axis=-1, keepdims=True)
        spread = jnp.mean(jnp.square(values - center), axis=-1, keepdims=True)
        scaled = (values - center) * lax.rsqrt(spread + 1e-06)
        normed = scaled * (1.0 + scale_ref[...].reshape(1, D)) + shift_ref[...].reshape(1, D)
        normed_ref[...] = normed.astype(BF16)
        lane = lane_ids((NOTE_ROWS, 128))
        note = jnp.zeros((NOTE_ROWS, 128), jnp.int32)
        for frame in range(FRAMES_DEV):
            note = jnp.where(lane == frame, times_ref[frame], note)
            note = jnp.where(lane == FRAMES_DEV + frame, levels_ref[frame], note)
        for slot in range(GROUPS):
            kv_out[slot, KV_ROWS:Q_AT] = note.astype(F32).astype(BF16)

    normed = normed_ref[...]
    queries = jnp.dot(normed, wq_ref[...], preferred_element_type=F32)
    keys = jnp.dot(normed, wk_ref[...], preferred_element_type=F32)
    values = jnp.dot(normed, wv_ref[...], preferred_element_type=F32)
    mine = lax.axis_index("seq") // PIECES
    half = ROWS // 2
    for odd in range(2):
        slot = jnp.bitwise_xor(2 * step + odd, mine)
        pair = slice(256, 384) if odd else slice(0, 128)
        middle = slice(128, 256)
        key_mid, value_mid, query_mid = keys[:, middle], values[:, middle], queries[:, middle]
        if odd:
            third = half_pair(pltpu.roll(key_mid, HD, 1), value_mid)
            query_third = half_pair(pltpu.roll(query_mid[:half], HD, 1), query_mid[half:])
        else:
            third = half_pair(key_mid, pltpu.roll(value_mid, HD, 1))
            query_third = half_pair(query_mid[:half], pltpu.roll(query_mid[half:], HD, 1))
        kv_out[slot, :ROWS] = keys[:, pair].astype(BF16)
        kv_out[slot, ROWS : 2 * ROWS] = values[:, pair].astype(BF16)
        kv_out[slot, 2 * ROWS : KV_ROWS] = third.astype(BF16)
        kv_out[slot, Q_AT : Q_AT + ROWS] = queries[:, pair].astype(BF16)
        kv_out[slot, Q_AT + ROWS :] = query_third.astype(BF16)


def project(frame_time, frame_level, tokens, shift, scale, w_qkv):
    width = 2 * BAND
    whole = lambda *shape: pl.BlockSpec(shape, lambda j: (0,) * len(shape))
    smem = pl.BlockSpec(memory_space=pltpu.SMEM)
    return pl.pallas_call(
        project_kernel,
        out_shape=jax.ShapeDtypeStruct((GROUPS, Q_AT + Q_ROWS, 128), BF16),
        grid=(2,),
        in_specs=[
            smem,
            smem,
            whole(ROWS, D),
            whole(D),
            whole(D),
            pl.BlockSpec((D, width), lambda j: (0, j)),
            pl.BlockSpec((D, width), lambda j: (0, 2 + j)),
            pl.BlockSpec((D, width), lambda j: (0, 4 + j)),
        ],
        out_specs=whole(GROUPS, Q_AT + Q_ROWS, 128),
        scratch_shapes=[pltpu.VMEM((ROWS, D), BF16)],
        compiler_params=pltpu.CompilerParams(vmem_limit_bytes=WIDE_VMEM),
        cost_estimate=pl.CostEstimate(
            flops=2 * ROWS * D * 3 * H * HD, bytes_accessed=2 * D * 3 * H * HD, transcendentals=0
        ),
    )(frame_time, frame_level, tokens, shift, scale, w_qkv, w_qkv, w_qkv)


def attend_kernel(*refs):
    kv_parts, q_parts, out_ref = refs[:TM], refs[TM : TM + 4], refs[TM + 4]
    kv_buf, q_buf, packed, v_flip, q_ext, excess, note_buf, notes, slot_of, place, count_to, sems, notes_vmem = refs[TM + 5 :]
    seq = lax.axis_index("seq")
    group, piece = seq // PIECES, seq % PIECES
    y_low, x_at = piece // 4, piece % 4

    note_copies = [
        pltpu.make_async_copy(kv_parts[n].at[0, KV_ROWS:Q_AT], note_buf.at[n], sems.at[n]) for n in range(TM)
    ]
    kv_copies = [pltpu.make_async_copy(kv_parts[n], kv_buf.at[n], sems.at[TM + n]) for n in range(TM)]
    q_copies = []
    for n, part in enumerate(q_parts):
        from_x = jnp.bitwise_and(x_at - n, 3)
        for flip in range(2):
            to = 4 * jnp.bitwise_xor(y_low, flip) + from_x
            q_copies.append(pltpu.make_async_copy(part.at[flip], q_buf.at[to], sems.at[2 * TM + 2 * n + flip]))
    for copy in note_copies + kv_copies + q_copies:
        copy.start()
    for copy in note_copies:
        copy.wait()
    kept = [note_buf[n].astype(F32).astype(jnp.int32)[:1] for n in range(TM)]
    notes_vmem[...] = jnp.concatenate(kept, axis=0)
    to_scalars = pltpu.make_async_copy(notes_vmem, notes, sems.at[4 * TM])
    to_scalars.start()
    to_scalars.wait()

    def time_at(i):
        return notes[i // FRAMES_DEV, i % FRAMES_DEV]

    def level_at(i):
        return notes[i // FRAMES_DEV, FRAMES_DEV + i % FRAMES_DEV]

    def chunks_of(level):
        return jnp.where(level == 0, GROUPS, jnp.where((level == 1) | (piece < 2), 1, 0))

    for i in range(FRAMES):
        slot_of[time_at(i)] = i

    def lay_out(t, used):
        i = slot_of[t]
        place[i] = used
        used = used + chunks_of(level_at(i))
        count_to[i] = used
        return used

    total = lax.fori_loop(0, FRAMES, lay_out, 0)
    tiles = jnp.maximum((total + CHUNKS_TILE - 1) // CHUNKS_TILE, 1)
    wide = (tiles + WIDE - 1) // WIDE

    def clear(c, carry):
        packed[c] = jnp.zeros((3, SHARD, 128), BF16)
        return carry

    lax.fori_loop(total, wide * WIDE * CHUNKS_TILE, clear, 0)

    for slot in range(TM):
        kv_copies[slot].wait()
        for frame in range(FRAMES_DEV):
            i = slot * FRAMES_DEV + frame
            to, here = place[i], chunks_of(level_at(i))

            def move(a, slot=slot, frame=frame, to=to):
                for plane in range(3):
                    row = plane * ROWS + frame * SHARD
                    packed[to + a, plane] = kv_buf[slot, jnp.bitwise_xor(a, group), row : row + SHARD]

            @pl.when(here > 0)
            def _(move=move):
                move(0)

            @pl.when(here > 1)
            def _(move=move):
                for a in range(1, GROUPS):
                    move(a)

    eye = (
        lax.broadcasted_iota(jnp.int32, (128, 128), 0) == lax.broadcasted_iota(jnp.int32, (128, 128), 1)
    ).astype(BF16)
    flip_dims = (((1,), (1,)), ((), ()))

    def flip_values(w, largest):
        tile = packed.at[pl.ds(w * WIDE * CHUNKS_TILE, WIDE * CHUNKS_TILE)]
        pair = lax.dot_general(
            eye, tile[:, 1].reshape(WIDE * KEY_TILE, 128), flip_dims, preferred_element_type=F32
        )
        third = lax.dot_general(
            eye[HD:], tile[:, 2].reshape(WIDE * KEY_TILE, 128), flip_dims, preferred_element_type=F32
        )
        for head, rows in enumerate((pair[:HD], pair[HD:], third)):
            for n in range(WIDE):
                part = rows[:, n * KEY_TILE : (n + 1) * KEY_TILE]
                v_flip[w * WIDE + n, head, :HD] = part.astype(BF16)
                v_flip[w * WIDE + n, head, HD:] = jnp.ones((SUM_ROWS, KEY_TILE), BF16)
                largest = jnp.maximum(largest, jnp.abs(part))
        return largest

    largest = lax.fori_loop(0, wide, flip_values, jnp.zeros((HD, KEY_TILE), F32))
    largest = jnp.max(jnp.max(largest, axis=0, keepdims=True), axis=1, keepdims=True)
    power = jnp.clip(jnp.floor(jnp.log2(largest)), -100.0, 100.0)
    grow = jnp.exp2(HEAD_ROOM - power)
    for copy in q_copies:
        copy.wait()
    excess[...] = jnp.zeros((8, QUERY_TILE), F32)

    key_row = lax.broadcasted_iota(jnp.int32, (KEY_TILE, QUERY_TILE), 0)

    def score_tile(c, head, limit=None):
        k_tile = packed[pl.ds(c * CHUNKS_TILE, CHUNKS_TILE), 2 if head == 2 else 0].reshape(KEY_TILE, 128)
        scores = lax.dot_general(k_tile, q_ext[head], flip_dims, preferred_element_type=F32) * SCALE
        return scores if limit is None else jnp.where(key_row < limit, scores, MASKED)

    def weigh(c, head, weights):
        return jnp.dot(v_flip[c, head], weights.astype(BF16), preferred_element_type=F32)

    def tall_max(scores):
        return jnp.max(scores.reshape(KEY_TILE // 8, 8, QUERY_TILE), axis=0)

    def place_queries(a, frame):
        shards = q_buf.at[:, jnp.bitwise_xor(a, group)]
        pair = shards[:, SHARD * frame : SHARD * (frame + 1)].reshape(QUERY_TILE, 128).astype(F32)
        low = ROWS + SHARD * (frame % 2)
        third = shards[:, low : low + SHARD].reshape(QUERY_TILE, 128).astype(F32)
        if frame // 2:
            third = pltpu.roll(third, HD, 1)
        none = jnp.zeros_like(pair)
        q_ext[0] = half_pair(pair, none).astype(BF16)
        q_ext[1] = half_pair(none, pair).astype(BF16)
        q_ext[2] = half_pair(third, none).astype(BF16)

    def write(a, frame, head, top, acc):
        sums = acc[HD : HD + 1]
        some = sums > 0.0
        out = acc[:HD] * jnp.where(some, grow / sums, 0.0)
        rest = jnp.where(some, top + jnp.log2(sums), LOWEST)
        digits = []
        for digit in range(DIGITS):
            unit = 2.0 ** (DIGIT_BITS * (2 - digit))
            whole = jnp.floor(rest * (1.0 / unit) + 0.5)
            rest = rest - whole * unit
            digits.append(whole)
        digits += [jnp.broadcast_to(power, (1, QUERY_TILE))] + [jnp.zeros_like(rest)] * 2
        rows = jnp.concatenate([out] + digits, axis=0)
        lanes = slice(SHARD * frame, SHARD * (frame + 1))
        for part in range(QUERY_TILE // 128):
            block = rows[:, 128 * part : 128 * (part + 1)]
            for sub in range(128 // SHARD):
                shift = (SHARD * (frame - sub)) % 128
                turned = pltpu.roll(block, shift, 1) if shift else block
                home = PIECES * a + 128 // SHARD * part + sub
                out_ref[home, HEAD_ROWS * head : HEAD_ROWS * (head + 1), lanes] = turned[:, lanes]

    def plan(frame):
        query_tiles = jnp.where(level_at(frame) == 0, GROUPS, 1)
        chunks = count_to[frame]
        key_tiles = jnp.maximum((chunks + CHUNKS_TILE - 1) // CHUNKS_TILE, 1)
        return query_tiles, key_tiles, (chunks - (key_tiles - 1) * CHUNKS_TILE) * SHARD

    for frame in range(FRAMES_DEV):
        query_tiles, key_tiles, last_rows = plan(frame)

        def one_query_tile(a, carry, frame=frame, key_tiles=key_tiles, last_rows=last_rows):
            place_queries(a, frame)
            full = key_tiles - 1
            first = [score_tile(full, head, last_rows) for head in range(3)]
            tops = [jnp.maximum(jnp.max(scores, axis=0, keepdims=True), TOP_START) for scores in first]
            first = [jnp.exp2(scores - top) for scores, top in zip(first, tops)]
            state = []
            for head in range(3):
                state.append(weigh(full, head, first[head]))
                state.append(jnp.broadcast_to(tops[head], (8, QUERY_TILE)))

            def key_steps(count):
                def run(c, state):
                    state = list(state)
                    items = [(count * c + n, head) for n in range(count) for head in range(3)]
                    scores = [score_tile(tile, head) for tile, head in items]
                    weights = [
                        jnp.exp2(one - tops[head]).astype(BF16) for one, (_, head) in zip(scores, items)
                    ]
                    for (tile, head), one, weight in zip(items, scores, weights):
                        state[2 * head] = state[2 * head] + weigh(tile, head, weight)
                        state[2 * head + 1] = jnp.maximum(state[2 * head + 1], tall_max(one))
                    return tuple(state)

                return run

            state = lax.fori_loop(0, full // 4, key_steps(4), tuple(state))
            state = lax.fori_loop(full // 4 * 2, full // 2, key_steps(2), state)
            state = lax.fori_loop(full // 2 * 2, full, key_steps(1), state)
            over = excess[...]
            for head in range(3):
                write(a, frame, head, tops[head], state[2 * head])
                over = jnp.maximum(over, state[2 * head + 1] - tops[head])
            excess[...] = over
            return carry

        lax.fori_loop(0, query_tiles, one_query_tile, 0)

    @pl.when(jnp.max(excess[...]) > EXCESS)
    def _():
        for frame in range(FRAMES_DEV):
            query_tiles, key_tiles, last_rows = plan(frame)

            def redo(a, carry, frame=frame, key_tiles=key_tiles, last_rows=last_rows):
                place_queries(a, frame)
                for head in range(3):

                    def one_key_tile(c, state, head=head):
                        top, acc = state
                        scores = score_tile(c, head, jnp.where(c == key_tiles - 1, last_rows, KEY_TILE))
                        new_top = jnp.maximum(top, jnp.max(scores, axis=0, keepdims=True))
                        acc = acc * jnp.exp2(top - new_top) + weigh(c, head, jnp.exp2(scores - new_top))
                        return new_top, acc

                    start = (jnp.full((1, QUERY_TILE), TOP_START, F32), jnp.zeros((V_ROWS, QUERY_TILE), F32))
                    top, acc = lax.fori_loop(0, key_tiles, one_key_tile, start)
                    write(a, frame, head, top, acc)
                return carry

            lax.fori_loop(0, query_tiles, redo, 0)


def attend(kv_parts, q_parts):
    hbm = pl.BlockSpec(memory_space=pl.ANY)
    vmem = pl.BlockSpec(memory_space=pltpu.VMEM)
    return pl.pallas_call(
        attend_kernel,
        out_shape=jax.ShapeDtypeStruct((32, MSG_ROWS, 128), F32),
        in_specs=[hbm] * (TM + 4),
        out_specs=vmem,
        scratch_shapes=[
            pltpu.VMEM((TM, GROUPS, Q_AT, 128), BF16),
            pltpu.VMEM((PIECES, GROUPS, Q_ROWS, 128), BF16),
            pltpu.VMEM((MAX_CHUNKS, 3, SHARD, 128), BF16),
            pltpu.VMEM((MAX_TILES, 3, V_ROWS, KEY_TILE), BF16),
            pltpu.VMEM((3, QUERY_TILE, 128), BF16),
            pltpu.VMEM((8, QUERY_TILE), F32),
            pltpu.VMEM((TM, NOTE_ROWS, 128), BF16),
            pltpu.SMEM((TM, 128), jnp.int32),
            pltpu.SMEM((FRAMES,), jnp.int32),
            pltpu.SMEM((FRAMES,), jnp.int32),
            pltpu.SMEM((FRAMES,), jnp.int32),
            pltpu.SemaphoreType.DMA((4 * TM + 1,)),
            pltpu.VMEM((TM, 128), jnp.int32),
        ],
        compiler_params=pltpu.CompilerParams(vmem_limit_bytes=VMEM_BYTES),
        cost_estimate=pl.CostEstimate(flops=10**10, bytes_accessed=10**7, transcendentals=10**7),
    )(*kv_parts, *q_parts)


def finish_kernel(levels_ref, home_ref, w_ref, gate_ref, out_ref, attn_ref):
    for group in range(GROUPS):
        base = 2 * BAND * (group // 2)
        if group % 2:
            places = (base + 4 * HD, base + 5 * HD, base + 3 * HD)
        else:
            places = (base, base + HD, base + 2 * HD)
        for head in range(3):
            at = HEAD_ROWS * head
            sizes, shrink = [], []
            for piece in range(PIECES):
                rows = home_ref[PIECES * group + piece, at + HD : at + HEAD_ROWS]
                size = None
                for digit in reversed(range(DIGITS)):
                    term = rows[digit : digit + 1] * 2.0 ** (DIGIT_BITS * (2 - digit))
                    size = term if size is None else size + term
                sizes.append(size)
                shrink.append(jnp.exp2(rows[DIGITS : DIGITS + 1] - HEAD_ROOM))
            best = sizes[0]
            for size in sizes[1:]:
                best = jnp.maximum(best, size)
            shares = [jnp.exp2(size - best) for size in sizes]
            norm = shares[0]
            for share in shares[1:]:
                norm = norm + share
            norm = 1.0 / norm
            acc = None
            for piece in range(PIECES):
                part = home_ref[PIECES * group + piece, at : at + HD] * (shares[piece] * norm * shrink[piece])
                acc = part if acc is None else acc + part
            attn_ref[places[head] : places[head] + HD] = acc.astype(BF16)
    mixed = lax.dot_general(
        attn_ref[...], w_ref[...], (((0,), (0,)), ((), ())), preferred_element_type=F32
    ) * gate_ref[...].reshape(1, D)
    for frame in range(FRAMES_DEV):
        rows = slice(SHARD * frame, SHARD * (frame + 1))
        limit = jnp.right_shift(jnp.int32(SHARD * 32), 2 * levels_ref[frame])
        used = lax.axis_index("seq") * SHARD < limit
        out_ref[rows] = jnp.where(used, mixed[rows], 0.0).astype(BF16)


def finish(frame_level, home, w_out, gate):
    vmem = pl.BlockSpec(memory_space=pltpu.VMEM)
    return pl.pallas_call(
        finish_kernel,
        out_shape=jax.ShapeDtypeStruct((ROWS, D), BF16),
        in_specs=[pl.BlockSpec(memory_space=pltpu.SMEM), vmem, vmem, vmem],
        out_specs=vmem,
        scratch_shapes=[pltpu.VMEM((H * HD, ROWS), BF16)],
        compiler_params=pltpu.CompilerParams(vmem_limit_bytes=VMEM_BYTES),
    )(frame_level, home, w_out, gate)


def permute(x, axis, to):
    return lax.ppermute(x, axis, [(i, to(i)) for i in range(lax.axis_size(axis))])


def other_core(i):
    return i ^ 1


def along_z(k):
    return lambda i: ((i >> 1) + k) % 4 * 2 + (i & 1)


def along_x(k):
    return lambda i: (i & ~3) | ((i + k) & 3)


def forward(i):
    return along_z(-1 if i & 1 else 1)(i)


def spread_frames(x, beside):
    below = permute(x, "tm", along_z(1))
    above = permute(x, "tm", along_z(-1))
    below, above, *beside = lax.optimization_barrier((below, above, *beside))
    core = lax.axis_index("tm") & 1
    far = permute(jnp.where(core == 0, below, above), "tm", forward)
    parts = []
    for one in (x, above, far, below):
        parts += [one, permute(one, "tm", other_core)]
    return parts, beside


def spread_queries(x):
    near = jnp.stack([x, permute(x, "seq", lambda i: i ^ 4)])
    return [near] + [permute(near, "seq", along_x(k)) for k in (1, 2, 3)]


def to_groups(x):
    return [x[0]] + [permute(x[k], "seq", lambda i, k=k: i ^ (8 * k)) for k in range(1, GROUPS)]


def per_device(tokens, mod_shift, mod_scale, out_gate, w_qkv, w_out, frame_time, frame_level):
    message = project(frame_time, frame_level, tokens.reshape(ROWS, D), mod_shift, mod_scale, w_qkv)
    parts = to_groups(message)
    kv_block = jnp.stack([part[:Q_AT] for part in parts])
    q_block = jnp.stack([part[Q_AT:] for part in parts])
    message = attend(*spread_frames(kv_block, spread_queries(q_block)))
    home = lax.all_to_all(message.astype(jnp.float16), "seq", split_axis=0, concat_axis=0, tiled=True)
    out = finish(frame_level, home.astype(F32), w_out, out_gate)
    return out.reshape(FRAMES_DEV, SHARD, D)


def solution(mesh):
    placed = (P("tm", "seq", None), P(), P(), P(), P(), P(), P("tm"), P("tm"))
    return jax.shard_map(
        per_device, mesh=mesh, in_specs=placed, out_specs=P("tm", "seq", None), check_vma=False
    )
```
